256 devices in a mesh: dp: 32 (over x, z), mp: 8 (over y, core).
Axes of the slice: x: 4, y: 4, z: 8, core: 2. Of those that a mesh axis runs over, the one named last changes fastest.
Arguments:
- hidden_acts: bfloat16 [16384, 16384], P('dp', 'mp'), may hold values from -40 to 40
- out_grads: bfloat16 [16384, 2048], P(('dp', 'mp')), may hold values from -40 to 40
- left_stats: float32 [8, 64, 512, 512], P('mp', 'dp'), may hold values from -1 to 40, as said below
- right_stats: float32 [8, 64, 512, 512], P('mp', 'dp'), may hold values from -1 to 40, as said below
- block_owner: int32 [16], replicated, may hold values from 0 to 31, as said below
- block_slot: int32 [16], replicated, may hold values from 0 to 1, as said below
Outputs:
- update: bfloat16 [8, 16, 512, 512], P('mp', None, 'dp')
The draws below stay inside these ranges and needn't reach their ends.
Inputs may be any that keep to these rules, and one draw needn't show every extreme that they name: `block_owner`: with block_slot, no two blocks share an (owner, slot) pair; an owner with a block in slot s has blocks in every lower slot; some owner holds 2 blocks. `block_slot`: the block's place among its owner's blocks. `left_stats`: each [512, 512] matrix is symmetric, with a positive diagonal entry larger than the sum of magnitudes of the rest of its row. `right_stats`: each [512, 512] matrix is symmetric, with a positive diagonal entry larger than the sum of magnitudes of the rest of its row.
All inputs are finite; a program needn't handle non-finite values. Where the reference program divides by a largest or mean magnitude, that divisor is 1e-20 or more.
Results may differ from the reference program's by a relative error of at most 0.0044.
The reference program's roundings to bfloat16 on the way (of `grads`) count: a program that leaves them out, or rounds other values in their place, can miss the bound.
Values may be sent and summed in bfloat16 or wider, within the bound.
A program may use at most 128 MiB of HBM per device.

```python
import math
import jax
import jax.numpy as jnp
from jax import lax

B = 512
GC = 4
CAP = 2
ITERS = 2
TOK_DEV = 512
GR = 4
NBLK = 16
TOKENS = 16384
N_DP = 32
N_MP = 8


def spread_factor(key, shape):
    return 10.0 ** (jax.random.uniform(key, shape, jnp.float32) - 0.5)


def stat_matrices(key, ratio, coupling):
    key_diag, key_off = jax.random.split(key)
    shape = (N_MP, N_DP * CAP, B, B)
    diagonal = ratio ** jax.random.uniform(key_diag, (N_MP, N_DP * CAP, B), jnp.float32)
    noise = jax.random.uniform(key_off, shape, jnp.float32, -1.0, 1.0)
    symmetric = 0.5 * (noise + jnp.swapaxes(noise, -1, -2))
    root_diag = jnp.sqrt(diagonal)
    offdiag = coupling * symmetric * root_diag[..., :, None] * root_diag[..., None, :] / B
    identity = jnp.eye(B, dtype=jnp.float32)
    return offdiag * (1.0 - identity) + identity * diagonal[..., :, None]


def assignment(key):
    key_owner, key_count, key_order = jax.random.split(key, 3)
    owners = jax.random.permutation(key_owner, N_DP).astype(jnp.int32)
    where_last = jnp.argmax((owners == N_DP - 1).astype(jnp.int32))
    first_owner = owners[0]
    owners = owners.at[where_last].set(first_owner)
    owners = owners.at[0].set(N_DP - 1)
    doubles = jax.random.randint(key_count, (), 1, NBLK // CAP + 1)
    entry = jnp.arange(NBLK)
    paired = entry < CAP * doubles
    single = jnp.clip(entry - (CAP - 1) * doubles, 0, N_DP - 1)
    owner_list = jnp.where(paired, owners[entry // CAP], owners[single])
    slot_list = jnp.where(paired, entry % CAP, 0)
    order = jax.random.permutation(key_order, NBLK)
    return (owner_list[order].astype(jnp.int32), slot_list[order].astype(jnp.int32))


def draw_hidden_acts(key, part):
    key = jax.random.fold_in(key, 3)
    key_base, key_rows, key_cols = jax.random.split(key, 3)
    shape = (TOKENS, N_MP * GR * B)
    values = jnp.clip(jax.random.normal(key_base, shape, jnp.float32), -4.0, 4.0)
    values = values * spread_factor(key_rows, (shape[0], 1)) * spread_factor(key_cols, (1, shape[1]))
    return values.astype(jnp.bfloat16)


def draw_out_grads(key, part):
    key = jax.random.fold_in(key, 4)
    key_base, key_rows, key_cols = jax.random.split(key, 3)
    shape = (TOKENS, GC * B)
    values = jnp.clip(jax.random.normal(key_base, shape, jnp.float32), -4.0, 4.0)
    values = values * spread_factor(key_rows, (shape[0], 1)) * spread_factor(key_cols, (1, shape[1]))
    return values.astype(jnp.bfloat16)


def draw_left_stats(key, part):
    key = jax.random.fold_in(key, 5)
    return stat_matrices(key, 30.0, 0.3)


def draw_right_stats(key, part):
    key = jax.random.fold_in(key, 7)
    return stat_matrices(key, 30.0, 0.3)


def draw_block_owner(key, part):
    owner_list, slot_list = assignment(key)
    return owner_list


def draw_block_slot(key, part):
    owner_list, slot_list = assignment(key)
    return slot_list


def setup_inputs(seed: int = 0) -> dict:
    seeds = jax.random.split(jax.random.key(seed), 7)
    return {
        "hidden_acts": draw_hidden_acts(jax.random.fold_in(seeds[6], 71), 0),
        "out_grads": draw_out_grads(jax.random.fold_in(seeds[6], 71), 0),
        "left_stats": draw_left_stats(jax.random.fold_in(seeds[6], 71), 0),
        "right_stats": draw_right_stats(jax.random.fold_in(seeds[6], 71), 0),
        "block_owner": draw_block_owner(jax.random.fold_in(seeds[6], 71), 0),
        "block_slot": draw_block_slot(jax.random.fold_in(seeds[6], 71), 0),
    }


def inverse_root(matrix):
    scaling = 1.0 / (jnp.max(lax.optimization_barrier(jnp.sum(jnp.abs(matrix), axis=1))) + 1e-06)
    current = matrix * scaling
    identity = jnp.eye(B, dtype=jnp.float32)
    inverse = identity
    for sweep in range(ITERS):
        polish = 1.25 * identity - 0.25 * current
        if sweep == 0:
            inverse = polish
        else:
            inverse = jnp.dot(inverse, polish, precision=lax.Precision.HIGHEST)
        if sweep + 1 < ITERS:
            square = jnp.dot(polish, polish, precision=lax.Precision.HIGHEST)
            fourth = jnp.dot(square, square, precision=lax.Precision.HIGHEST)
            current = jnp.dot(fourth, current, precision=lax.Precision.HIGHEST)
    return inverse

def precondition(triple):
    gradient, left_prev, right_prev = triple
    left_total = left_prev + jnp.dot(gradient, gradient.T, preferred_element_type=jnp.float32)
    right_total = right_prev + jnp.dot(gradient.T, gradient, preferred_element_type=jnp.float32)
    widened = gradient.astype(jnp.float32)
    result = jnp.dot(inverse_root(left_total), widened, precision=lax.Precision.HIGHEST)
    result = jnp.dot(result, inverse_root(right_total), precision=lax.Precision.HIGHEST)
    return (result * lax.rsqrt(jnp.mean(result * result) + 1e-06)).astype(jnp.bfloat16)

def reference(hidden_acts, out_grads, left_stats, right_stats, block_owner, block_slot):
    factor = 1.0 / math.sqrt(B * TOKENS)

    def group_term(summed, group):
        offset = group * TOK_DEV
        hidden = lax.dynamic_slice_in_dim(hidden_acts, offset, TOK_DEV, 0)
        cotangent = lax.dynamic_slice_in_dim(out_grads, offset, TOK_DEV, 0)
        term = jnp.dot(hidden.T, cotangent, preferred_element_type=jnp.float32) * factor
        return (summed + term, None)
    initial = jnp.zeros((N_MP * GR * B, GC * B), jnp.float32)
    summed, _ = lax.scan(group_term, initial, jnp.arange(N_DP, dtype=jnp.int32))
    grads = summed.astype(jnp.bfloat16).reshape(N_MP, GR, B, GC, B)
    grads = grads.transpose(0, 1, 3, 2, 4).reshape(N_MP * NBLK, B, B)
    position = (block_owner * CAP + block_slot).astype(jnp.int32)
    left_prev = jnp.take(left_stats, position, axis=1).reshape(N_MP * NBLK, B, B)
    right_prev = jnp.take(right_stats, position, axis=1).reshape(N_MP * NBLK, B, B)
    updates = lax.map(precondition, (grads, left_prev, right_prev))
    return updates.reshape(N_MP, NBLK, B, B)
```

```python
import math

import jax
import jax.numpy as jnp
from jax import lax
from jax.experimental import pallas as pl
from jax.experimental.pallas import tpu as pltpu
from jax.sharding import PartitionSpec as P

B = 512
CAP = 2
NX = 4
NZ = 8
NY = 4
DP = NX * NZ
MP = 2 * NY
GR = 4
GC = 4
NBLK = GR * GC
TOK = 512
SUB = TOK // MP
WIDTH = B // DP
XROWS = B // NX
F32 = jnp.float32
BF16 = jnp.bfloat16
MESH = pl.DeviceIdType.MESH


def dot(a, b, ca=1, cb=0):
    return lax.dot_general(a, b, (((ca,), (cb,)), ((), ())), preferred_element_type=F32)


def root_less_identity(matrix, eye):
    column_sums = jnp.sum(jnp.abs(matrix), axis=0, keepdims=True)
    scaling = 1.0 / (jnp.max(column_sums) + 1e-06)
    e1 = 0.25 * eye - (0.25 * scaling) * matrix
    e1b = e1.astype(BF16)
    e2 = dot(e1b, e1b)
    e2b = e2.astype(BF16)
    e34 = dot(e2b, (4.75 * e1 + e2).astype(BF16))
    return e1 + 2.5 * e2 + dot(e2b, (7.5 * e1 + 8.75 * e2 + e34).astype(BF16))


def body_kernel(
    hid, og, left, right, owner, slot, out,
    cg, hx, ht, tile, cw, ccw, g16, send, mine, upd, arr, lbuf, rbuf, chosen,
    loc, a_s, a_r, h_s, h_r, b1_s, b1_r, b2_s, b2_r, s_s, s_r, r_s, r_r, g_s, g_r, u_s, u_r,
):
    i = lax.axis_index("dp")
    m = lax.axis_index("mp")
    x = i // NZ
    z = i % NZ
    core = m % 2
    sib = m + 1 - 2 * core
    up = (m + 2) % MP
    down = (m + MP - 2) % MP
    far = (m + 4) % MP
    factor = 1.0 / math.sqrt(B * TOK * DP)

    def remote(src, dst, ss, rs, dp, mp):
        return pltpu.make_async_remote_copy(
            src_ref=src, dst_ref=dst, send_sem=ss, recv_sem=rs,
            device_id=(dp, mp), device_id_type=MESH,
        )

    def wait(ref, sem):
        pltpu.make_async_copy(ref, ref, sem).wait()

    def peer(d):
        return ((x + d // NZ) % NX) * NZ + (z + d % NZ) % NZ

    def xpeer(d):
        return ((x + d) % NX) * NZ + z

    znext = x * NZ + (z + 1) % NZ
    zprev = x * NZ + (z + NZ - 1) % NZ

    def cols(r, xx):
        return pl.ds(pl.multiple_of(r * B + xx * XROWS, XROWS), XROWS)

    stat_copies = [
        pltpu.make_async_copy(left.at[0], lbuf, loc.at[0]),
        pltpu.make_async_copy(right.at[0], rbuf, loc.at[1]),
    ]
    own_copies = [
        pltpu.make_async_copy(og.at[:, pl.ds(c * B, B)], cg.at[c, x, m], loc.at[2 + c])
        for c in range(GC)
    ]
    hid_copies = [
        pltpu.make_async_copy(
            hid.at[:, cols(r, x)], hx.at[x, :, pl.ds(r * XROWS, XROWS)], loc.at[6 + r]
        )
        for r in range(GR)
    ]
    for copy in own_copies + hid_copies:
        copy.start()

    barrier = pltpu.get_barrier_semaphore()

    def greet(d, carry):
        pl.semaphore_signal(barrier, inc=1, device_id=(peer(d), m), device_id_type=MESH)
        return carry

    for other in (up, down, sib):
        pl.semaphore_signal(barrier, inc=1, device_id=(i, other), device_id_type=MESH)
    lax.fori_loop(1, DP, greet, 0)
    pl.semaphore_wait(barrier, DP - 1 + 3)

    def start_a(c):
        for d in (1, 3, 2):
            remote(
                og.at[:, pl.ds(c * B, B)], cg.at[c, x, m], a_s.at[c], a_r.at[c], xpeer(d), m
            ).start()

    def start_h():
        for r in range(GR):
            for d in (1, 3, 2):
                remote(
                    hid.at[:, cols(r, (x + d) % NX)],
                    hx.at[x, :, pl.ds(r * XROWS, XROWS)],
                    h_s.at[d - 1], h_r.at[d - 1], xpeer(d), m,
                ).start()

    def b1(c, k):
        return remote(
            cg.at[c, :, m], cg.at[c, :, m], b1_s.at[c, k], b1_r.at[c, k], i, (up, down)[k]
        )

    def b2(c, k):
        half = pl.ds(2 * k, 2)
        group = (down, up)[k]
        return remote(
            cg.at[c, half, group], cg.at[c, half, group],
            b2_s.at[c, k], b2_r.at[c, k], i, (up, down)[k],
        )

    def share(c, n):
        group = (m, down, up, far)[n]
        return remote(
            cg.at[c, :, group], cg.at[c, :, group], s_s.at[c, n], s_r.at[c, n], i, sib
        )

    def stage1(c):
        own_copies[c].wait()
        wait(cg.at[c, pl.ds(0, 3), 0], a_r.at[c])
        b1(c, 0).start()
        b1(c, 1).start()
        share(c, 0).start()

    def stage2(c):
        for k in (0, 1):
            b1(c, k).wait_recv()
            b2(c, k).start()
            share(c, 1 + k).start()

    def stage3(c):
        for k in (0, 1):
            b2(c, k).wait_recv()
        share(c, 3).start()

    def prepare_hidden():
        for copy in hid_copies:
            copy.wait()
        for d in (1, 3, 2):
            wait(hx.at[0], h_r.at[d - 1])
        for n in range(NX):
            ht[:, pl.ds(n * TOK, TOK)] = hx[n].T

    def hop(ring, c, k, k_ref):
        buf = (cw, ccw)[ring]
        target = (znext, zprev)[ring]
        if k == 0:
            rows = pl.ds(2 * ring, 2)
            return remote(
                tile.at[c, (z + 4) % NZ, rows], buf.at[c, 0, rows],
                r_s.at[ring, c, 0], r_r.at[ring, c, 0], target, m,
            )
        return remote(
            buf.at[c, k - 1], buf.at[c, k], r_s.at[ring, c, k], r_r.at[ring, c, k], target, m
        )

    def stage4(c):
        for n in range(4):
            share(c, n).wait_recv()
        total = dot(ht[...], cg[c].reshape(NX * TOK, B))
        for r in range(GR):
            for zz in range(NZ):
                start = r * XROWS + zz * WIDTH
                tile[c, zz, r] = total[start : start + WIDTH]
        hop(0, c, 0, None).start()
        hop(1, c, 0, None).start()

    def ring_step(c, k):
        for ring in (0, 1):
            buf = (cw, ccw)[ring]
            hop(ring, c, k, None).wait_recv()
            chunk = (z + 3 - k) % NZ if ring == 0 else (z + NZ - 3 + k) % NZ
            if k == 0:
                mine_rows, other_rows = (pl.ds(2 * ring, 2), pl.ds(2 - 2 * ring, 2))
                buf[c, 0, mine_rows] = buf[c, 0, mine_rows] + tile[c, chunk, mine_rows]
                buf[c, 0, other_rows] = tile[c, chunk, other_rows]
            else:
                buf[c, k] = buf[c, k] + tile[c, chunk]
            hop(ring, c, k + 1, None).start()

    def ring_end(c):
        for ring in (0, 1):
            hop(ring, c, 3, None).wait_recv()
        total = (tile[c, z] + cw[c, 3]) + ccw[c, 3]
        total = (total * factor).astype(BF16)
        for r in range(GR):
            g16[r * GC + c] = total[r]

    def find_chosen():
        positions = [owner[j] * CAP + slot[j] for j in range(NBLK)]

        def find(p, carry):
            found = jnp.int32(0)
            for j in range(NBLK):
                found = jnp.where(positions[j] == p, j, found)
            chosen[p] = found
            return carry

        lax.fori_loop(0, DP * CAP, find, 0)

    start_a(0)
    start_a(1)
    start_h()
    start_a(2)
    start_a(3)
    for copy in stat_copies:
        copy.start()
    find_chosen()

    ready = (21.0, 25.0, 33.0, 35.0)
    plan = [
        (3.0, stage1, (0,)), (4.0, stage1, (1,)), (8.0, stage2, (0,)), (9.0, stage1, (2,)),
        (13.0, stage2, (1,)), (14.0, stage1, (3,)), (16.0, stage3, (0,)),
        (20.0, prepare_hidden, ()),
        (21.5, stage2, (2,)), (24.0, stage3, (1,)), (29.0, stage2, (3,)), (31.5, stage3, (2,)),
        (34.0, stage3, (3,)),
    ]
    for c in range(GC):
        plan.append((ready[c], stage4, (c,)))
        for k in range(3):
            plan.append((ready[c] + 4.0 * (k + 1), ring_step, (c, k)))
        plan.append((ready[c] + 16.0, ring_end, (c,)))
    for _, action, args in sorted(plan, key=lambda entry: entry[0]):
        action(*args)

    rows_me = pl.ds(pl.multiple_of(i * WIDTH, WIDTH), WIDTH)
    for s in range(CAP):

        def deliver(d, carry):
            e = peer(d)
            send[s, e] = g16[chosen[e * CAP + s]]
            remote(
                send.at[s, e], mine.at[s, rows_me], g_s.at[s], g_r.at[s], e, m
            ).start()
            return carry

        lax.fori_loop(1, DP, deliver, 0)
        mine[s, rows_me] = g16[chosen[i * CAP + s]]
    for copy in stat_copies:
        copy.wait()

    all_but_one = pl.ds(0, (DP - 1) * WIDTH)

    def refresh(s, carry):
        wait(mine.at[s, all_but_one], g_r.at[s])
        row = lax.broadcasted_iota(jnp.int32, (B, B), 0)
        col = lax.broadcasted_iota(jnp.int32, (B, B), 1)
        eye = jnp.where(row == col, 1.0, 0.0).astype(F32)
        grad = mine[s]
        wl = root_less_identity(lbuf[s] + dot(grad, grad, 1, 1), eye).astype(BF16)
        wr = root_less_identity(rbuf[s] + dot(grad, grad, 0, 0), eye).astype(BF16)
        half = grad.astype(F32) + dot(wl, grad)
        full = half + dot(half.astype(BF16), wr)
        scale = lax.rsqrt(jnp.sum(full * full) * (1.0 / (B * B)) + 1e-06)
        upd[s] = (full * scale).astype(BF16)

        def give(d, inner):
            e = peer(d)
            rows = pl.ds(pl.multiple_of(e * WIDTH, WIDTH), WIDTH)
            remote(upd.at[s, rows], arr.at[s, i], u_s.at[s], u_r.at[s], e, m).start()
            return inner

        lax.fori_loop(1, DP, give, 0)
        arr[s, i] = upd[s, rows_me]
        return carry

    lax.fori_loop(0, CAP, refresh, 0)

    for s in range(CAP):
        wait(arr.at[s, pl.ds(0, DP - 1)], u_r.at[s])
    for j in range(NBLK):
        out[j] = arr[slot[j], owner[j]]

    for s in range(CAP):
        wait(mine.at[s, all_but_one], g_s.at[s])
        wait(mine.at[s, all_but_one], u_s.at[s])
    for d in range(3):
        wait(hx.at[0], h_s.at[d])
    for c in range(GC):
        wait(cg.at[c, pl.ds(0, 3), 0], a_s.at[c])
        for k in range(2):
            b1(c, k).wait_send()
            b2(c, k).wait_send()
        for n in range(4):
            share(c, n).wait_send()
        for ring in range(2):
            for k in range(4):
                hop(ring, c, k, None).wait_send()


def body(hidden_acts, out_grads, left_stats, right_stats, block_owner, block_slot):
    hbm = pl.BlockSpec(memory_space=pl.ANY)
    smem = pl.BlockSpec(memory_space=pltpu.SMEM)
    vmem = pl.BlockSpec(memory_space=pltpu.VMEM)
    dma = pltpu.SemaphoreType.DMA
    result = pl.pallas_call(
        body_kernel,
        out_shape=jax.ShapeDtypeStruct((NBLK, WIDTH, B), BF16),
        in_specs=[hbm, hbm, hbm, hbm, smem, smem],
        out_specs=vmem,
        scratch_shapes=[
            pltpu.VMEM((GC, NX, MP, SUB, B), BF16),
            pltpu.VMEM((NX, TOK, GR * XROWS), BF16),
            pltpu.VMEM((GR * XROWS, NX * TOK), BF16),
            pltpu.VMEM((GC, NZ, GR, WIDTH, B), F32),
            pltpu.VMEM((GC, 4, GR, WIDTH, B), F32),
            pltpu.VMEM((GC, 4, GR, WIDTH, B), F32),
            pltpu.VMEM((NBLK, WIDTH, B), BF16),
            pltpu.VMEM((CAP, DP, WIDTH, B), BF16),
            pltpu.VMEM((CAP, B, B), BF16),
            pltpu.VMEM((CAP, B, B), BF16),
            pltpu.VMEM((CAP, DP, WIDTH, B), BF16),
            pltpu.VMEM((CAP, B, B), F32),
            pltpu.VMEM((CAP, B, B), F32),
            pltpu.SMEM((DP * CAP,), jnp.int32),
            dma((10,)),
            dma((GC,)), dma((GC,)),
            dma((3,)), dma((3,)),
            dma((GC, 2)), dma((GC, 2)),
            dma((GC, 2)), dma((GC, 2)),
            dma((GC, 4)), dma((GC, 4)),
            dma((2, GC, 4)), dma((2, GC, 4)),
            dma((CAP,)), dma((CAP,)),
            dma((CAP,)), dma((CAP,)),
        ],
        compiler_params=pltpu.CompilerParams(
            collective_id=0, has_side_effects=True, vmem_limit_bytes=60 * 1024 * 1024
        ),
        cost_estimate=pl.CostEstimate(
            flops=10 * 10**9, bytes_accessed=7 * 10**6, transcendentals=0
        ),
    )(hidden_acts, out_grads, left_stats, right_stats, block_owner, block_slot)
    return result[None]


def solution(mesh):
    in_specs = (
        P("dp", "mp"),
        P(("dp", "mp"), None),
        P("mp", "dp", None, None),
        P("mp", "dp", None, None),
        P(),
        P(),
    )
    out_specs = P("mp", None, "dp", None)
    return jax.shard_map(body, mesh=mesh, in_specs=in_specs, out_specs=out_specs, check_vma=False)
```

```python
import math

import jax
import jax.numpy as jnp
from jax import lax
from jax.experimental import pallas as pl
from jax.experimental.pallas import tpu as pltpu
from jax.sharding import PartitionSpec as P

B = 512
CAP = 2
NX = 4
NZ = 8
NY = 4
DP = NX * NZ
MP = 2 * NY
GR = 4
GC = 4
NBLK = GR * GC
TOK = 512
SUB = TOK // MP
WIDTH = B // DP
XROWS = B // NX
F32 = jnp.float32
BF16 = jnp.bfloat16
MESH = pl.DeviceIdType.MESH

A_TIMES = (0.0, 0.02, 4.55, 11.0)
OWN_TIMES = (0.01, 0.03, 0.04, 13.6)
H_TIMES = (6.0, 9.1, 15.0, 18.6)
FIND_TIME = 1.0
HID_TIME = 12.2
STAT_TIME = 37.0
RELAY_TIMES = (4.4, 4.9, 8.6, 15.6)
NEAR_TIMES = (4.5, 9.0, 13.5, 20.0)
FAR_TIMES = (8.5, 11.1, 14.0, 20.5)
MIDDLE_TIMES = (
    (5.6, 10.5, 10.6, 12.5), (8.7, 13.0, 13.1, 14.5),
    (14.2, 19.0, 19.1, 21.0), (20.6, 25.5, 25.6, 27.5),
)
LAST_TIMES = (15.2, 18.5, 24.0, 31.0)
PREPARE_TIMES = (17.1, 29.0)
TILES = (
    (17.2, 0, 0), (21.2, 0, 1), (27.6, 0, 2), (29.1, 1, 0),
    (29.2, 1, 1), (30.5, 1, 2), (33.0, 0, 3), (33.7, 1, 3),
)
HOP_TIME = 1.35
HOP_DELAY = 1.7


def ring_order():
    waiting = [(t + 0.8, p, c, -1) for t, p, c in TILES]
    order, free = [], 0.0
    while waiting:
        waiting.sort()
        t, p, c, k = waiting.pop(0)
        if k >= 0:
            order.append((t, p, c, k))
        if k < 3:
            free = max(t, free) + (0.5 * HOP_TIME if k < 0 else HOP_TIME)
            waiting.append((free + HOP_DELAY, p, c, k + 1))
    return order


def dot(a, b, ca=1, cb=0):
    return lax.dot_general(a, b, (((ca,), (cb,)), ((), ())), preferred_element_type=F32)


def root_less_identity(matrix, eye):
    column_sums = jnp.sum(jnp.abs(matrix), axis=0, keepdims=True)
    scaling = 1.0 / (jnp.max(column_sums) + 1e-06)
    e1 = 0.25 * eye - (0.25 * scaling) * matrix
    e1b = e1.astype(BF16)
    e2 = dot(e1b, e1b)
    e2b = e2.astype(BF16)
    e34 = dot(e2b, (4.75 * e1 + e2).astype(BF16))
    return e1 + 2.5 * e2 + dot(e2b, (7.5 * e1 + 8.75 * e2 + e34).astype(BF16))


def body_kernel(
    hid, og, left, right, owner, slot, out,
    cg, hx, ht, tile, cw, ccw, g16, send, mine, upd, arr, lbuf, rbuf, chosen,
    loc, a_s, a_r, h_s, h_r, b1_s, b1_r, b2_s, b2_r, s_s, s_r, r_s, r_r, g_s, g_r, u_s, u_r,
):
    i = lax.axis_index("dp")
    m = lax.axis_index("mp")
    x = i // NZ
    z = i % NZ
    core = m % 2
    sib = m + 1 - 2 * core
    up = (m + 2) % MP
    down = (m + MP - 2) % MP
    far = (m + 4) % MP
    factor = 1.0 / math.sqrt(B * TOK * DP)

    def remote(src, dst, ss, rs, dp, mp):
        return pltpu.make_async_remote_copy(
            src_ref=src, dst_ref=dst, send_sem=ss, recv_sem=rs,
            device_id=(dp, mp), device_id_type=MESH,
        )

    def wait(ref, sem):
        pltpu.make_async_copy(ref, ref, sem).wait()

    def peer(d):
        return ((x + d // NZ) % NX) * NZ + (z + d % NZ) % NZ

    def xpeer(d):
        return ((x + d) % NX) * NZ + z

    znext = x * NZ + (z + 1) % NZ
    zprev = x * NZ + (z + NZ - 1) % NZ

    def cols(r, xx):
        return pl.ds(pl.multiple_of(r * B + xx * XROWS, XROWS), XROWS)

    stat_copies = [
        pltpu.make_async_copy(left.at[0], lbuf, loc.at[0]),
        pltpu.make_async_copy(right.at[0], rbuf, loc.at[1]),
    ]
    own_copies = [
        pltpu.make_async_copy(og.at[:, pl.ds(c * B, B)], cg.at[c, x, m], loc.at[2 + c])
        for c in range(GC)
    ]
    hid_copies = [
        pltpu.make_async_copy(
            hid.at[:, cols(r, x)], hx.at[x, :, pl.ds(r * XROWS, XROWS)], loc.at[6 + r]
        )
        for r in range(GR)
    ]
    for copy in own_copies:
        copy.start()

    barrier = pltpu.get_barrier_semaphore()
    greeted = [(xpeer(d), m) for d in (1, 2, 3)]
    greeted += [(znext, m), (zprev, m), (i, up), (i, down), (i, sib)]
    for target in greeted:
        pl.semaphore_signal(barrier, inc=1, device_id=target, device_id_type=MESH)
    pl.semaphore_wait(barrier, len(greeted))

    def slab(q):
        return (x + q) % NX

    def a_copy(c, d):
        ss, rs = a_s.at[c, 3 - d], a_r.at[c, 3 - d]
        if d == 2:
            step = 1 + 2 * (c % 2)
            ref = cg.at[c, slab(4 - step), m]
            return remote(ref, ref, ss, rs, xpeer(step), m)
        return remote(og.at[:, pl.ds(c * B, B)], cg.at[c, x, m], ss, rs, xpeer(d), m)

    def h_copy(r, d):
        return remote(
            hid.at[:, cols(r, (x + d) % NX)], hx.at[x, :, pl.ds(r * XROWS, XROWS)],
            h_s.at[r, d - 1], h_r.at[r, d - 1], xpeer(d), m,
        )

    def b1(c, k, q):
        src = og.at[:, pl.ds(c * B, B)] if q == 0 else cg.at[c, slab(q), m]
        return remote(
            src, cg.at[c, slab(q), m], b1_s.at[c, k, q], b1_r.at[c, k, q], i, (up, down)[k]
        )

    def b2(c, q):
        k = q // 2
        ref = cg.at[c, slab(q), (down, up)[k]]
        return remote(ref, ref, b2_s.at[c, q], b2_r.at[c, q], i, (up, down)[k])

    def share(c, n):
        ref = cg.at[c, :, (m, down, up, far)[n]]
        return remote(ref, ref, s_s.at[c, n], s_r.at[c, n], i, sib)

    def send_a(c):
        for d in (1, 3):
            a_copy(c, d).start()

    def send_h(r):
        for d in (1, 3, 2):
            h_copy(r, d).start()

    def send_own(c):
        b1(c, 0, 0).start()
        b1(c, 1, 0).start()

    def relay(c):
        step = 1 + 2 * (c % 2)
        a_copy(c, step).wait_recv()
        a_copy(c, 2).start()

    def near(c):
        step = 1 + 2 * (c % 2)
        for d in (step, 4 - step):
            if d != step:
                a_copy(c, d).wait_recv()
            b1(c, 0, 4 - d).start()
            b1(c, 1, 4 - d).start()

    def far_one(c):
        a_copy(c, 2).wait_recv()
        b1(c, 0, 2).start()
        b1(c, 1, 2).start()
        own_copies[c].wait()
        share(c, 0).start()

    def middle(c, q):
        for k in (0, 1):
            b1(c, k, q).wait_recv()
            if k == q // 2:
                b2(c, q).start()
        if q == 2:
            share(c, 1).start()
            share(c, 2).start()

    def last(c):
        for q in range(NX):
            b2(c, q).wait_recv()
        share(c, 3).start()

    def prepare_hidden(p):
        for r in (2 * p, 2 * p + 1):
            hid_copies[r].wait()
            for d in (1, 3, 2):
                h_copy(r, d).wait_recv()
        half = pl.ds(2 * p * XROWS, 2 * XROWS)
        for n in range(NX):
            ht[half, pl.ds(n * TOK, TOK)] = hx[n, :, half].T

    def hop(ring, p, c, k):
        buf = (cw, ccw)[ring]
        target = (znext, zprev)[ring]
        ss, rs = r_s.at[ring, p, c, k], r_r.at[ring, p, c, k]
        if k == 0:
            r = 2 * p + ring
            return remote(tile.at[c, (z + 4) % NZ, r], buf.at[c, 0, r], ss, rs, target, m)
        pair = pl.ds(2 * p, 2)
        return remote(buf.at[c, k - 1, pair], buf.at[c, k, pair], ss, rs, target, m)

    seen = set()

    def multiply(p, c):
        if c not in seen:
            for n in range(4):
                share(c, n).wait_recv()
            seen.add(c)
        total = dot(ht[pl.ds(2 * p * XROWS, 2 * XROWS)], cg[c].reshape(NX * TOK, B))
        for r in range(2):
            for zz in range(NZ):
                start = r * XROWS + zz * WIDTH
                tile[c, zz, 2 * p + r] = total[start : start + WIDTH]
        hop(0, p, c, 0).start()
        hop(1, p, c, 0).start()

    def ring_step(p, c, k):
        for ring in (0, 1):
            buf = (cw, ccw)[ring]
            hop(ring, p, c, k).wait_recv()
            chunk = (z + 3 - k) % NZ if ring == 0 else (z + NZ - 3 + k) % NZ
            if k == 0:
                same, other = 2 * p + ring, 2 * p + 1 - ring
                buf[c, 0, same] = buf[c, 0, same] + tile[c, chunk, same]
                buf[c, 0, other] = tile[c, chunk, other]
            else:
                pair = pl.ds(2 * p, 2)
                buf[c, k, pair] = buf[c, k, pair] + tile[c, chunk, pair]
            hop(ring, p, c, k + 1).start()

    def ring_end(p, c):
        for ring in (0, 1):
            hop(ring, p, c, 3).wait_recv()
        pair = pl.ds(2 * p, 2)
        total = (tile[c, z, pair] + cw[c, 3, pair]) + ccw[c, 3, pair]
        total = (total * factor).astype(BF16)
        for r in range(2):
            g16[(2 * p + r) * GC + c] = total[r]

    def find_chosen():
        positions = [owner[j] * CAP + slot[j] for j in range(NBLK)]

        def find(p, carry):
            found = jnp.int32(0)
            for j in range(NBLK):
                found = jnp.where(positions[j] == p, j, found)
            chosen[p] = found
            return carry

        lax.fori_loop(0, DP * CAP, find, 0)

    def start_local(copies):
        for copy in copies:
            copy.start()

    plan = [(t, send_a, (c,)) for c, t in enumerate(A_TIMES)]
    plan += [(t, send_own, (c,)) for c, t in enumerate(OWN_TIMES)]
    plan += [(t, send_h, (r,)) for r, t in enumerate(H_TIMES)]
    plan += [(FIND_TIME, find_chosen, ()), (HID_TIME, start_local, (hid_copies,)), (STAT_TIME, start_local, (stat_copies,))]
    for c in range(GC):
        plan.append((RELAY_TIMES[c], relay, (c,)))
        plan.append((NEAR_TIMES[c], near, (c,)))
        plan.append((FAR_TIMES[c], far_one, (c,)))
        for q, t in zip((0, 3, 1, 2), MIDDLE_TIMES[c]):
            plan.append((t, middle, (c, q)))
        plan.append((LAST_TIMES[c], last, (c,)))
    plan += [(t, prepare_hidden, (p,)) for p, t in enumerate(PREPARE_TIMES)]
    for t, p, c in TILES:
        plan.append((t, multiply, (p, c)))
    for t, p, c, k in ring_order():
        plan.append((t, ring_step, (p, c, k)) if k < 3 else (t, ring_end, (p, c)))
    for _, action, args in sorted(plan, key=lambda entry: entry[0]):
        action(*args)

    rows_me = pl.ds(pl.multiple_of(i * WIDTH, WIDTH), WIDTH)
    for s in range(CAP):

        def deliver(d, carry):
            e = peer(d)
            send[s, e] = g16[chosen[e * CAP + s]]
            remote(
                send.at[s, e], mine.at[s, rows_me], g_s.at[s], g_r.at[s], e, m
            ).start()
            return carry

        lax.fori_loop(1, DP, deliver, 0)
        mine[s, rows_me] = g16[chosen[i * CAP + s]]
    for copy in stat_copies:
        copy.wait()

    all_but_one = pl.ds(0, (DP - 1) * WIDTH)

    def refresh(s, carry):
        wait(mine.at[s, all_but_one], g_r.at[s])
        row = lax.broadcasted_iota(jnp.int32, (B, B), 0)
        col = lax.broadcasted_iota(jnp.int32, (B, B), 1)
        eye = jnp.where(row == col, 1.0, 0.0).astype(F32)
        grad = mine[s]
        wl = root_less_identity(lbuf[s] + dot(grad, grad, 1, 1), eye).astype(BF16)
        wr = root_less_identity(rbuf[s] + dot(grad, grad, 0, 0), eye).astype(BF16)
        half = grad.astype(F32) + dot(wl, grad)
        full = half + dot(half.astype(BF16), wr)
        scale = lax.rsqrt(jnp.sum(full * full) * (1.0 / (B * B)) + 1e-06)
        upd[s] = (full * scale).astype(BF16)

        def give(d, inner):
            e = peer(d)
            rows = pl.ds(pl.multiple_of(e * WIDTH, WIDTH), WIDTH)
            remote(upd.at[s, rows], arr.at[s, i], u_s.at[s], u_r.at[s], e, m).start()
            return inner

        lax.fori_loop(1, DP, give, 0)
        arr[s, i] = upd[s, rows_me]
        return carry

    lax.fori_loop(0, CAP, refresh, 0)

    for s in range(CAP):
        wait(arr.at[s, pl.ds(0, DP - 1)], u_r.at[s])
    for j in range(NBLK):
        out[j] = arr[slot[j], owner[j]]

    for s in range(CAP):
        wait(mine.at[s, all_but_one], g_s.at[s])
        wait(mine.at[s, all_but_one], u_s.at[s])
    for c in range(GC):
        for d in range(1, NX):
            a_copy(c, d).wait_send()
            h_copy(c, d).wait_send()
        for q in range(NX):
            b1(c, 0, q).wait_send()
            b1(c, 1, q).wait_send()
            b2(c, q).wait_send()
            share(c, q).wait_send()
        for ring in range(2):
            for p in range(2):
                for k in range(4):
                    hop(ring, p, c, k).wait_send()


def body(hidden_acts, out_grads, left_stats, right_stats, block_owner, block_slot):
    hbm = pl.BlockSpec(memory_space=pl.ANY)
    smem = pl.BlockSpec(memory_space=pltpu.SMEM)
    vmem = pl.BlockSpec(memory_space=pltpu.VMEM)
    dma = pltpu.SemaphoreType.DMA
    result = pl.pallas_call(
        body_kernel,
        out_shape=jax.ShapeDtypeStruct((NBLK, WIDTH, B), BF16),
        in_specs=[hbm, hbm, hbm, hbm, smem, smem],
        out_specs=vmem,
        scratch_shapes=[
            pltpu.VMEM((GC, NX, MP, SUB, B), BF16),
            pltpu.VMEM((NX, TOK, GR * XROWS), BF16),
            pltpu.VMEM((GR * XROWS, NX * TOK), BF16),
            pltpu.VMEM((GC, NZ, GR, WIDTH, B), F32),
            pltpu.VMEM((GC, 4, GR, WIDTH, B), F32),
            pltpu.VMEM((GC, 4, GR, WIDTH, B), F32),
            pltpu.VMEM((NBLK, WIDTH, B), BF16),
            pltpu.VMEM((CAP, DP, WIDTH, B), BF16),
            pltpu.VMEM((CAP, B, B), BF16),
            pltpu.VMEM((CAP, B, B), BF16),
            pltpu.VMEM((CAP, DP, WIDTH, B), BF16),
            pltpu.VMEM((CAP, B, B), F32),
            pltpu.VMEM((CAP, B, B), F32),
            pltpu.SMEM((DP * CAP,), jnp.int32),
            dma((10,)),
            dma((GC, 3)), dma((GC, 3)),
            dma((GR, 3)), dma((GR, 3)),
            dma((GC, 2, NX)), dma((GC, 2, NX)),
            dma((GC, NX)), dma((GC, NX)),
            dma((GC, 4)), dma((GC, 4)),
            dma((2, 2, GC, 4)), dma((2, 2, GC, 4)),
            dma((CAP,)), dma((CAP,)),
            dma((CAP,)), dma((CAP,)),
        ],
        compiler_params=pltpu.CompilerParams(
            collective_id=0, has_side_effects=True, vmem_limit_bytes=60 * 1024 * 1024
        ),
        cost_estimate=pl.CostEstimate(
            flops=10 * 10**9, bytes_accessed=7 * 10**6, transcendentals=0
        ),
    )(hidden_acts, out_grads, left_stats, right_stats, block_owner, block_slot)
    return result[None]


def solution(mesh):
    in_specs = (
        P("dp", "mp"),
        P(("dp", "mp"), None),
        P("mp", "dp", None, None),
        P("mp", "dp", None, None),
        P(),
        P(),
    )
    out_specs = P("mp", None, "dp", None)
    return jax.shard_map(body, mesh=mesh, in_specs=in_specs, out_specs=out_specs, check_vma=False)
```

```python
import math

import jax
import jax.numpy as jnp
from jax import lax
from jax.experimental import pallas as pl
from jax.experimental.pallas import tpu as pltpu
from jax.sharding import PartitionSpec as P

B = 512
CAP = 2
NX = 4
NZ = 8
NY = 4
DP = NX * NZ
MP = 2 * NY
GR = 4
GC = 4
NBLK = GR * GC
TOK = 512
SUB = TOK // MP
WIDTH = B // DP
XROWS = B // NX
F32 = jnp.float32
BF16 = jnp.bfloat16
MESH = pl.DeviceIdType.MESH

A_TIMES = (0.0, 0.02, 0.04, 0.06)
OWN_TIMES = (0.01, 0.03, 0.05, 0.07)
H_TIMES = (7.5, 11.0, 13.05, 14.9)
FIND_TIME = 1.0
HID_TIME = 14.95
STAT_TIME = 50.0
RELAY_TIMES = (6.5, 6.65, 7.2, 7.4)
NEAR_TIMES = (6.6, 6.7, 13.1, 19.1)
FAR_TIMES = (9.5, 10.5, 15.3, 19.15)
MIDDLE_TIMES = (
    (8.0, 12.0, 12.1, 13.0), (10.6, 14.0, 14.1, 15.2),
    (20.2, 21.0, 21.1, 23.0), (23.1, 26.5, 26.6, 28.5),
)
LAST_TIMES = (15.0, 19.0, 25.0, 30.5)
PREPARE_TIMES = (18.0, 23.5)
TILES = (
    (18.1, 0, 0), (20.5, 0, 1), (23.6, 1, 0), (23.7, 1, 1),
    (27.0, 0, 2), (27.2, 1, 2), (33.0, 0, 3), (33.2, 1, 3),
)
HOP_TIME = 1.35
HOP_DELAY = 1.7


def ring_order():
    waiting = [(t + 0.8, p, c, -1) for t, p, c in TILES]
    order, free = [], 0.0
    while waiting:
        waiting.sort()
        t, p, c, k = waiting.pop(0)
        if k >= 0:
            order.append((t, p, c, k))
        if k < 3:
            free = max(t, free) + HOP_TIME * (0.25, 0.5, 1.0, 1.0)[k + 1]
            waiting.append((free + HOP_DELAY, p, c, k + 1))
    return order


def dot(a, b, ca=1, cb=0):
    return lax.dot_general(a, b, (((ca,), (cb,)), ((), ())), preferred_element_type=F32)


def root_less_identity(matrix, eye):
    column_sums = jnp.sum(jnp.abs(matrix), axis=0, keepdims=True)
    scaling = 1.0 / (jnp.max(column_sums) + 1e-06)
    e1 = 0.25 * eye - (0.25 * scaling) * matrix
    e1b = e1.astype(BF16)
    e2 = dot(e1b, e1b)
    e2b = e2.astype(BF16)
    e34 = dot(e2b, (4.75 * e1 + e2).astype(BF16))
    return e1 + 2.5 * e2 + dot(e2b, (7.5 * e1 + 8.75 * e2 + e34).astype(BF16))


def body_kernel(
    hid, og, left, right, owner, slot, out,
    cg, hx, ht, tile, cw, ccw, early, landed, g16, send, mine, upd, arr, lbuf, rbuf, chosen,
    loc, a_s, a_r, h_s, h_r, b1_s, b1_r, b2_s, b2_r, s_s, s_r, r_s, r_r, g_s, g_r, u_s, u_r,
):
    i = lax.axis_index("dp")
    m = lax.axis_index("mp")
    x = i // NZ
    z = i % NZ
    core = m % 2
    sib = m + 1 - 2 * core
    up = (m + 2) % MP
    down = (m + MP - 2) % MP
    far = (m + 4) % MP
    factor = 1.0 / math.sqrt(B * TOK * DP)

    def remote(src, dst, ss, rs, dp, mp):
        return pltpu.make_async_remote_copy(
            src_ref=src, dst_ref=dst, send_sem=ss, recv_sem=rs,
            device_id=(dp, mp), device_id_type=MESH,
        )

    def wait(ref, sem):
        pltpu.make_async_copy(ref, ref, sem).wait()

    def peer(d):
        return ((x + d // NZ) % NX) * NZ + (z + d % NZ) % NZ

    def xpeer(d):
        return ((x + d) % NX) * NZ + z

    znext = x * NZ + (z + 1) % NZ
    zprev = x * NZ + (z + NZ - 1) % NZ

    def cols(r, xx):
        return pl.ds(pl.multiple_of(r * B + xx * XROWS, XROWS), XROWS)

    stat_copies = [
        pltpu.make_async_copy(left.at[0], lbuf, loc.at[0]),
        pltpu.make_async_copy(right.at[0], rbuf, loc.at[1]),
    ]
    own_copies = [
        pltpu.make_async_copy(og.at[:, pl.ds(c * B, B)], cg.at[c, x, m], loc.at[2 + c])
        for c in range(GC)
    ]
    hid_copies = [
        pltpu.make_async_copy(
            hid.at[:, cols(r, x)], hx.at[x, :, pl.ds(r * XROWS, XROWS)], loc.at[6 + r]
        )
        for r in range(GR)
    ]
    for copy in own_copies:
        copy.start()

    barrier = pltpu.get_barrier_semaphore()
    greeted = [(xpeer(d), m) for d in (1, 2, 3)]
    greeted += [(znext, m), (zprev, m), (i, up), (i, down), (i, sib)]
    for target in greeted:
        pl.semaphore_signal(barrier, inc=1, device_id=target, device_id_type=MESH)
    pl.semaphore_wait(barrier, len(greeted))

    def slab(q):
        return (x + q) % NX

    def a_copy(c, d):
        ss, rs = a_s.at[c, 3 - d], a_r.at[c, 3 - d]
        if d == 2:
            step = 1 + 2 * (c % 2)
            ref = cg.at[c, slab(4 - step), m]
            return remote(ref, ref, ss, rs, xpeer(step), m)
        return remote(og.at[:, pl.ds(c * B, B)], cg.at[c, x, m], ss, rs, xpeer(d), m)

    def h_copy(r, d):
        return remote(
            hid.at[:, cols(r, (x + d) % NX)], hx.at[x, :, pl.ds(r * XROWS, XROWS)],
            h_s.at[r, d - 1], h_r.at[r, d - 1], xpeer(d), m,
        )

    def b1(c, k, q):
        src = og.at[:, pl.ds(c * B, B)] if q == 0 else cg.at[c, slab(q), m]
        return remote(
            src, cg.at[c, slab(q), m], b1_s.at[c, k, q], b1_r.at[c, k, q], i, (up, down)[k]
        )

    def b2(c, q):
        k = q // 2
        ref = cg.at[c, slab(q), (down, up)[k]]
        return remote(ref, ref, b2_s.at[c, q], b2_r.at[c, q], i, (up, down)[k])

    def share(c, n):
        ref = cg.at[c, :, (m, down, up, far)[n]]
        return remote(ref, ref, s_s.at[c, n], s_r.at[c, n], i, sib)

    def send_a(c):
        for d in (1, 3):
            a_copy(c, d).start()

    def send_h(r):
        for d in (1, 3, 2):
            h_copy(r, d).start()

    def send_own(c):
        b1(c, 0, 0).start()
        b1(c, 1, 0).start()

    def relay(c):
        step = 1 + 2 * (c % 2)
        a_copy(c, step).wait_recv()
        a_copy(c, 2).start()

    def near(c):
        step = 1 + 2 * (c % 2)
        for d in (step, 4 - step):
            if d != step:
                a_copy(c, d).wait_recv()
            b1(c, 0, 4 - d).start()
            b1(c, 1, 4 - d).start()

    def far_one(c):
        a_copy(c, 2).wait_recv()
        b1(c, 0, 2).start()
        b1(c, 1, 2).start()
        own_copies[c].wait()
        share(c, 0).start()

    def middle(c, q):
        for k in (0, 1):
            b1(c, k, q).wait_recv()
            if k == q // 2:
                b2(c, q).start()
        if q == 2:
            share(c, 1).start()
            share(c, 2).start()

    def last(c):
        for q in range(NX):
            b2(c, q).wait_recv()
        share(c, 3).start()

    def prepare_hidden(p):
        for r in (2 * p, 2 * p + 1):
            hid_copies[r].wait()
            for d in (1, 3, 2):
                h_copy(r, d).wait_recv()
        half = pl.ds(2 * p * XROWS, 2 * XROWS)
        for n in range(NX):
            ht[half, pl.ds(n * TOK, TOK)] = hx[n, :, half].T

    def hop(ring, p, c, k):
        buf = (cw, ccw)[ring]
        target = (znext, zprev)[ring]
        ss, rs = r_s.at[ring, p, c, k], r_r.at[ring, p, c, k]
        if k < 2:
            rows = pl.ds(2 * p, 2) if k else 2 * p + ring
            return remote(
                early.at[ring, c, k, rows], landed.at[ring, c, k, rows], ss, rs, target, m
            )
        pair = pl.ds(2 * p, 2)
        return remote(buf.at[c, k - 2, pair], buf.at[c, k - 1, pair], ss, rs, target, m)

    seen = set()

    def multiply(p, c):
        if c not in seen:
            for n in range(4):
                share(c, n).wait_recv()
            seen.add(c)
        total = dot(ht[pl.ds(2 * p * XROWS, 2 * XROWS)], cg[c].reshape(NX * TOK, B))
        for r in range(2):
            for zz in range(NZ):
                start = r * XROWS + zz * WIDTH
                tile[c, zz, 2 * p + r] = total[start : start + WIDTH]
        for ring in (0, 1):
            row = 2 * p + ring
            early[ring, c, 0, row] = tile[c, (z + 4) % NZ, row].astype(BF16)
            hop(ring, p, c, 0).start()

    def ring_step(p, c, k):
        for ring in (0, 1):
            buf = (cw, ccw)[ring]
            hop(ring, p, c, k).wait_recv()
            chunk = (z + 3 - k) % NZ if ring == 0 else (z + NZ - 3 + k) % NZ
            pair = pl.ds(2 * p, 2)
            if k == 0:
                same, other = 2 * p + ring, 2 * p + 1 - ring
                summed = landed[ring, c, 0, same].astype(F32) + tile[c, chunk, same]
                early[ring, c, 1, same] = summed.astype(BF16)
                early[ring, c, 1, other] = tile[c, chunk, other].astype(BF16)
            elif k == 1:
                buf[c, 0, pair] = landed[ring, c, 1, pair].astype(F32) + tile[c, chunk, pair]
            else:
                buf[c, 1, pair] = buf[c, 1, pair] + tile[c, chunk, pair]
            hop(ring, p, c, k + 1).start()

    def ring_end(p, c):
        for ring in (0, 1):
            hop(ring, p, c, 3).wait_recv()
        pair = pl.ds(2 * p, 2)
        total = (tile[c, z, pair] + cw[c, 2, pair]) + ccw[c, 2, pair]
        total = (total * factor).astype(BF16)
        for r in range(2):
            g16[(2 * p + r) * GC + c] = total[r]

    def find_chosen():
        positions = [owner[j] * CAP + slot[j] for j in range(NBLK)]

        def find(p, carry):
            found = jnp.int32(0)
            for j in range(NBLK):
                found = jnp.where(positions[j] == p, j, found)
            chosen[p] = found
            return carry

        lax.fori_loop(0, DP * CAP, find, 0)

    def start_local(copies):
        for copy in copies:
            copy.start()

    plan = [(t, send_a, (c,)) for c, t in enumerate(A_TIMES)]
    plan += [(t, send_own, (c,)) for c, t in enumerate(OWN_TIMES)]
    plan += [(t, send_h, (r,)) for r, t in enumerate(H_TIMES)]
    plan += [(FIND_TIME, find_chosen, ()), (HID_TIME, start_local, (hid_copies,)), (STAT_TIME, start_local, (stat_copies,))]
    for c in range(GC):
        plan.append((RELAY_TIMES[c], relay, (c,)))
        plan.append((NEAR_TIMES[c], near, (c,)))
        plan.append((FAR_TIMES[c], far_one, (c,)))
        for q, t in zip((0, 3, 1, 2), MIDDLE_TIMES[c]):
            plan.append((t, middle, (c, q)))
        plan.append((LAST_TIMES[c], last, (c,)))
    plan += [(t, prepare_hidden, (p,)) for p, t in enumerate(PREPARE_TIMES)]
    for t, p, c in TILES:
        plan.append((t, multiply, (p, c)))
    for t, p, c, k in ring_order():
        plan.append((t, ring_step, (p, c, k)) if k < 3 else (t, ring_end, (p, c)))
    for _, action, args in sorted(plan, key=lambda entry: entry[0]):
        action(*args)

    rows_me = pl.ds(pl.multiple_of(i * WIDTH, WIDTH), WIDTH)
    for s in range(CAP):

        def deliver(d, carry):
            e = peer(d)
            send[s, e] = g16[chosen[e * CAP + s]]
            remote(
                send.at[s, e], mine.at[s, rows_me], g_s.at[s], g_r.at[s], e, m
            ).start()
            return carry

        lax.fori_loop(1, DP, deliver, 0)
        if s == 0:
            wait(mine.at[s, pl.ds(0, (DP - 1) * WIDTH)], g_s.at[s])
        mine[s, rows_me] = g16[chosen[i * CAP + s]]
    for copy in stat_copies:
        copy.wait()

    all_but_one = pl.ds(0, (DP - 1) * WIDTH)

    def refresh(s, carry):
        wait(mine.at[s, all_but_one], g_r.at[s])
        row = lax.broadcasted_iota(jnp.int32, (B, B), 0)
        col = lax.broadcasted_iota(jnp.int32, (B, B), 1)
        eye = jnp.where(row == col, 1.0, 0.0).astype(F32)
        grad = mine[s]
        wl = root_less_identity(lbuf[s] + dot(grad, grad, 1, 1), eye).astype(BF16)
        wr = root_less_identity(rbuf[s] + dot(grad, grad, 0, 0), eye).astype(BF16)
        half = grad.astype(F32) + dot(wl, grad)
        full = half + dot(half.astype(BF16), wr)
        scale = lax.rsqrt(jnp.sum(full * full) * (1.0 / (B * B)) + 1e-06)
        upd[s] = (full * scale).astype(BF16)

        def give(d, inner):
            e = peer(d)
            rows = pl.ds(pl.multiple_of(e * WIDTH, WIDTH), WIDTH)
            remote(upd.at[s, rows], arr.at[s, i], u_s.at[s], u_r.at[s], e, m).start()
            return inner

        lax.fori_loop(1, DP, give, 0)
        arr[s, i] = upd[s, rows_me]
        return carry

    lax.fori_loop(0, CAP, refresh, 0)

    for s in range(CAP):
        wait(arr.at[s, pl.ds(0, DP - 1)], u_r.at[s])
    for j in range(NBLK):
        out[j] = arr[slot[j], owner[j]]

    for s in range(CAP):
        if s > 0:
            wait(mine.at[s, all_but_one], g_s.at[s])
        wait(mine.at[s, all_but_one], u_s.at[s])
    for c in range(GC):
        for d in range(1, NX):
            a_copy(c, d).wait_send()
            h_copy(c, d).wait_send()
        for q in range(NX):
            b1(c, 0, q).wait_send()
            b1(c, 1, q).wait_send()
            b2(c, q).wait_send()
            share(c, q).wait_send()
        for ring in range(2):
            for p in range(2):
                for k in range(4):
                    hop(ring, p, c, k).wait_send()


def body(hidden_acts, out_grads, left_stats, right_stats, block_owner, block_slot):
    hbm = pl.BlockSpec(memory_space=pl.ANY)
    smem = pl.BlockSpec(memory_space=pltpu.SMEM)
    vmem = pl.BlockSpec(memory_space=pltpu.VMEM)
    dma = pltpu.SemaphoreType.DMA
    result = pl.pallas_call(
        body_kernel,
        out_shape=jax.ShapeDtypeStruct((NBLK, WIDTH, B), BF16),
        in_specs=[hbm, hbm, hbm, hbm, smem, smem],
        out_specs=vmem,
        scratch_shapes=[
            pltpu.VMEM((GC, NX, MP, SUB, B), BF16),
            pltpu.VMEM((NX, TOK, GR * XROWS), BF16),
            pltpu.VMEM((GR * XROWS, NX * TOK), BF16),
            pltpu.VMEM((GC, NZ, GR, WIDTH, B), F32),
            pltpu.VMEM((GC, 3, GR, WIDTH, B), F32),
            pltpu.VMEM((GC, 3, GR, WIDTH, B), F32),
            pltpu.VMEM((2, GC, 2, GR, WIDTH, B), BF16),
            pltpu.VMEM((2, GC, 2, GR, WIDTH, B), BF16),
            pltpu.VMEM((NBLK, WIDTH, B), BF16),
            pltpu.VMEM((CAP, DP, WIDTH, B), BF16),
            pltpu.VMEM((CAP, B, B), BF16),
            pltpu.VMEM((CAP, B, B), BF16),
            pltpu.VMEM((CAP, DP, WIDTH, B), BF16),
            pltpu.VMEM((CAP, B, B), F32),
            pltpu.VMEM((CAP, B, B), F32),
            pltpu.SMEM((DP * CAP,), jnp.int32),
            dma((10,)),
            dma((GC, 3)), dma((GC, 3)),
            dma((GR, 3)), dma((GR, 3)),
            dma((GC, 2, NX)), dma((GC, 2, NX)),
            dma((GC, NX)), dma((GC, NX)),
            dma((GC, 4)), dma((GC, 4)),
            dma((2, 2, GC, 4)), dma((2, 2, GC, 4)),
            dma((CAP,)), dma((CAP,)),
            dma((CAP,)), dma((CAP,)),
        ],
        compiler_params=pltpu.CompilerParams(
            collective_id=0, has_side_effects=True, vmem_limit_bytes=60 * 1024 * 1024
        ),
        cost_estimate=pl.CostEstimate(
            flops=10 * 10**9, bytes_accessed=7 * 10**6, transcendentals=0
        ),
    )(hidden_acts, out_grads, left_stats, right_stats, block_owner, block_slot)
    return result[None]


def solution(mesh):
    in_specs = (
        P("dp", "mp"),
        P(("dp", "mp"), None),
        P("mp", "dp", None, None),
        P("mp", "dp", None, None),
        P(),
        P(),
    )
    out_specs = P("mp", None, "dp", None)
    return jax.shard_map(body, mesh=mesh, in_specs=in_specs, out_specs=out_specs, check_vma=False)
```

```python
import math

import jax
import jax.numpy as jnp
from jax import lax
from jax.experimental import pallas as pl
from jax.experimental.pallas import tpu as pltpu
from jax.sharding import PartitionSpec as P

B = 512
CAP = 2
NX = 4
NZ = 8
NY = 4
DP = NX * NZ
MP = 2 * NY
GR = 4
GC = 4
NBLK = GR * GC
TOK = 512
SUB = TOK // MP
WIDTH = B // DP
XROWS = B // NX
F32 = jnp.float32
BF16 = jnp.bfloat16
MESH = pl.DeviceIdType.MESH

A_TIMES = (0.0, 0.02, 0.04, 0.06)
OWN_TIMES = (0.01, 0.03, 0.05, 0.07)
H_TIMES = (7.5, 11.0, 13.05, 14.9)
FIND_TIME = 1.0
HID_TIME = 14.95
STAT_TIME = 55.0
RELAY_TIMES = (6.5, 6.65, 7.2, 7.4)
NEAR_TIMES = (6.6, 6.7, 12.2, 25.3)
FAR_TIMES = (9.5, 10.5, 13.05, 25.35)
MIDDLE_TIMES = (
    (8.0, 12.0, 12.1, 13.0), (10.6, 14.0, 14.1, 15.2),
    (27.0, 27.1, 27.2, 29.0), (29.1, 33.5, 33.6, 35.5),
)
LAST_TIMES = (19.0, 25.2, 33.0, 38.5)
PREPARE_TIMES = (23.0, 32.0)
TILES = (
    (24.0, 0, 0), (26.5, 0, 1), (32.1, 1, 0), (32.2, 1, 1),
    (35.0, 0, 2), (35.1, 1, 2), (41.0, 0, 3), (41.2, 1, 3),
)
HOP_TIMES = (0.37, 0.72, 1.4, 1.4)
HOP_DELAY = 2.4
LEAD = 1.0


def ring_order():
    waiting = [(t + 0.8, p, c, -1) for t, p, c in TILES]
    order, free, now = [], 0.0, 0.0
    while waiting:
        now = max(now, free - LEAD, min(waiting)[0])
        entry = min((e for e in waiting if e[0] <= now), key=lambda e: (e[3], e[0]))
        waiting.remove(entry)
        _, p, c, k = entry
        if k >= 0:
            order.append((now, p, c, k))
        if k < 3:
            free = max(now, free) + HOP_TIMES[k + 1]
            waiting.append((free + HOP_DELAY, p, c, k + 1))
    return order


def dot(a, b, ca=1, cb=0):
    return lax.dot_general(a, b, (((ca,), (cb,)), ((), ())), preferred_element_type=F32)


def split(value):
    top = value.astype(BF16)
    return top, (value - top.astype(F32)).astype(BF16)


def root_less_identity(matrix, eye):
    column_sums = jnp.sum(jnp.abs(matrix), axis=0, keepdims=True)
    scaling = 1.0 / (jnp.max(column_sums) + 1e-06)
    e1 = 0.25 * eye - (0.25 * scaling) * matrix
    e1b = e1.astype(BF16)
    e2 = dot(e1b, e1b)
    e2b = e2.astype(BF16)
    e34 = dot(e2b, (4.75 * e1 + e2).astype(BF16))
    return e1 + 2.5 * e2 + dot(e2b, (7.5 * e1 + 8.75 * e2 + e34).astype(BF16))


def body_kernel(
    hid, og, left, right, owner, slot, out,
    cg, hx, ht, tile, cw, ccw, early, landed, g16, send, mine, upd, arr, lbuf, rbuf, chosen,
    loc, a_s, a_r, h_s, h_r, b1_s, b1_r, b2_s, b2_r, s_s, s_r, r_s, r_r, g_s, g_r, u_s, u_r,
):
    i = lax.axis_index("dp")
    m = lax.axis_index("mp")
    x = i // NZ
    z = i % NZ
    core = m % 2
    sib = m + 1 - 2 * core
    up = (m + 2) % MP
    down = (m + MP - 2) % MP
    far = (m + 4) % MP
    factor = 1.0 / math.sqrt(B * TOK * DP)

    def remote(src, dst, ss, rs, dp, mp):
        return pltpu.make_async_remote_copy(
            src_ref=src, dst_ref=dst, send_sem=ss, recv_sem=rs,
            device_id=(dp, mp), device_id_type=MESH,
        )

    def wait(ref, sem):
        pltpu.make_async_copy(ref, ref, sem).wait()

    def peer(d):
        return ((x + d // NZ) % NX) * NZ + (z + d % NZ) % NZ

    def xpeer(d):
        return ((x + d) % NX) * NZ + z

    znext = x * NZ + (z + 1) % NZ
    zprev = x * NZ + (z + NZ - 1) % NZ

    def cols(r, xx):
        return pl.ds(pl.multiple_of(r * B + xx * XROWS, XROWS), XROWS)

    stat_copies = [
        pltpu.make_async_copy(left.at[0], lbuf, loc.at[0]),
        pltpu.make_async_copy(right.at[0], rbuf, loc.at[1]),
    ]
    own_copies = [
        pltpu.make_async_copy(og.at[:, pl.ds(c * B, B)], cg.at[c, x, m], loc.at[2 + c])
        for c in range(GC)
    ]
    hid_copies = [
        pltpu.make_async_copy(
            hid.at[:, cols(r, x)], hx.at[x, :, pl.ds(r * XROWS, XROWS)], loc.at[6 + r]
        )
        for r in range(GR)
    ]
    for copy in own_copies:
        copy.start()

    barrier = pltpu.get_barrier_semaphore()
    greeted = [(xpeer(d), m) for d in (1, 2, 3)]
    greeted += [(znext, m), (zprev, m), (i, up), (i, down), (i, sib)]
    for target in greeted:
        pl.semaphore_signal(barrier, inc=1, device_id=target, device_id_type=MESH)
    pl.semaphore_wait(barrier, len(greeted))

    def slab(q):
        return (x + q) % NX

    def a_copy(c, d):
        ss, rs = a_s.at[c, 3 - d], a_r.at[c, 3 - d]
        if d == 2:
            step = 1 + 2 * (c % 2)
            ref = cg.at[c, slab(4 - step), m]
            return remote(ref, ref, ss, rs, xpeer(step), m)
        return remote(og.at[:, pl.ds(c * B, B)], cg.at[c, x, m], ss, rs, xpeer(d), m)

    def h_copy(r, d):
        return remote(
            hid.at[:, cols(r, (x + d) % NX)], hx.at[x, :, pl.ds(r * XROWS, XROWS)],
            h_s.at[r, d - 1], h_r.at[r, d - 1], xpeer(d), m,
        )

    def b1(c, k, q):
        src = og.at[:, pl.ds(c * B, B)] if q == 0 else cg.at[c, slab(q), m]
        return remote(
            src, cg.at[c, slab(q), m], b1_s.at[c, k, q], b1_r.at[c, k, q], i, (up, down)[k]
        )

    def b2(c, q):
        k = q // 2
        ref = cg.at[c, slab(q), (down, up)[k]]
        return remote(ref, ref, b2_s.at[c, q], b2_r.at[c, q], i, (up, down)[k])

    def share(c, n):
        ref = cg.at[c, :, (m, down, up, far)[n]]
        return remote(ref, ref, s_s.at[c, n], s_r.at[c, n], i, sib)

    def send_a(c):
        for d in (1, 3):
            a_copy(c, d).start()

    def send_h(r):
        for d in (1, 3, 2):
            h_copy(r, d).start()

    def send_own(c):
        b1(c, 0, 0).start()
        b1(c, 1, 0).start()

    def relay(c):
        step = 1 + 2 * (c % 2)
        a_copy(c, step).wait_recv()
        a_copy(c, 2).start()

    def near(c):
        step = 1 + 2 * (c % 2)
        for d in (step, 4 - step):
            if d != step:
                a_copy(c, d).wait_recv()
            b1(c, 0, 4 - d).start()
            b1(c, 1, 4 - d).start()

    def far_one(c):
        a_copy(c, 2).wait_recv()
        b1(c, 0, 2).start()
        b1(c, 1, 2).start()
        own_copies[c].wait()
        share(c, 0).start()

    def middle(c, q):
        for k in (0, 1):
            b1(c, k, q).wait_recv()
            if k == q // 2:
                b2(c, q).start()
        if q == 2:
            share(c, 1).start()
            share(c, 2).start()

    def last(c):
        for q in range(NX):
            b2(c, q).wait_recv()
        share(c, 3).start()

    def prepare_hidden(p):
        for r in (2 * p, 2 * p + 1):
            hid_copies[r].wait()
            for d in (1, 3, 2):
                h_copy(r, d).wait_recv()
        half = pl.ds(2 * p * XROWS, 2 * XROWS)
        for n in range(NX):
            ht[half, pl.ds(n * TOK, TOK)] = hx[n, :, half].T

    def hop(ring, p, c, k):
        buf = (cw, ccw)[ring]
        target = (znext, zprev)[ring]
        ss, rs = r_s.at[ring, p, c, k], r_r.at[ring, p, c, k]
        if k < 2:
            rows = pl.ds(2 * p, 2) if k else 2 * p + ring
            return remote(
                early.at[ring, c, k, rows], landed.at[ring, c, k, rows], ss, rs, target, m
            )
        pair = pl.ds(2 * p, 2)
        return remote(buf.at[c, k - 2, pair], buf.at[c, k - 1, pair], ss, rs, target, m)

    seen = set()

    def multiply(p, c):
        if c not in seen:
            for n in range(4):
                share(c, n).wait_recv()
            seen.add(c)
        total = dot(ht[pl.ds(2 * p * XROWS, 2 * XROWS)], cg[c].reshape(NX * TOK, B))
        for r in range(2):
            for zz in range(NZ):
                start = r * XROWS + zz * WIDTH
                tile[c, zz, 2 * p + r] = total[start : start + WIDTH]
        for ring in (0, 1):
            row = 2 * p + ring
            early[ring, c, 0, row] = tile[c, (z + 4) % NZ, row].astype(BF16)
            hop(ring, p, c, 0).start()

    def ring_step(p, c, k):
        for ring in (0, 1):
            buf = (cw, ccw)[ring]
            hop(ring, p, c, k).wait_recv()
            chunk = (z + 3 - k) % NZ if ring == 0 else (z + NZ - 3 + k) % NZ
            pair = pl.ds(2 * p, 2)
            if k == 0:
                same, other = 2 * p + ring, 2 * p + 1 - ring
                summed = landed[ring, c, 0, same].astype(F32) + tile[c, chunk, same]
                early[ring, c, 1, same] = summed.astype(BF16)
                early[ring, c, 1, other] = tile[c, chunk, other].astype(BF16)
            elif k == 1:
                buf[c, 0, pair] = landed[ring, c, 1, pair].astype(F32) + tile[c, chunk, pair]
            else:
                buf[c, 1, pair] = buf[c, 1, pair] + tile[c, chunk, pair]
            hop(ring, p, c, k + 1).start()

    def ring_end(p, c):
        for ring in (0, 1):
            hop(ring, p, c, 3).wait_recv()
        pair = pl.ds(2 * p, 2)
        total = (tile[c, z, pair] + cw[c, 2, pair]) + ccw[c, 2, pair]
        total = (total * factor).astype(BF16)
        for r in range(2):
            g16[(2 * p + r) * GC + c] = total[r]

    def find_chosen():
        positions = [owner[j] * CAP + slot[j] for j in range(NBLK)]

        def find(p, carry):
            found = jnp.int32(0)
            for j in range(NBLK):
                found = jnp.where(positions[j] == p, j, found)
            chosen[p] = found
            return carry

        lax.fori_loop(0, DP * CAP, find, 0)

    def start_local(copies):
        for copy in copies:
            copy.start()

    plan = [(t, send_a, (c,)) for c, t in enumerate(A_TIMES)]
    plan += [(t, send_own, (c,)) for c, t in enumerate(OWN_TIMES)]
    plan += [(t, send_h, (r,)) for r, t in enumerate(H_TIMES)]
    plan += [(FIND_TIME, find_chosen, ()), (HID_TIME, start_local, (hid_copies,)), (STAT_TIME, start_local, (stat_copies,))]
    for c in range(GC):
        plan.append((RELAY_TIMES[c], relay, (c,)))
        plan.append((NEAR_TIMES[c], near, (c,)))
        plan.append((FAR_TIMES[c], far_one, (c,)))
        for q, t in zip((0, 3, 1, 2), MIDDLE_TIMES[c]):
            plan.append((t, middle, (c, q)))
        plan.append((LAST_TIMES[c], last, (c,)))
    plan += [(t, prepare_hidden, (p,)) for p, t in enumerate(PREPARE_TIMES)]
    for t, p, c in TILES:
        plan.append((t, multiply, (p, c)))
    for t, p, c, k in ring_order():
        plan.append((t, ring_step, (p, c, k)) if k < 3 else (t, ring_end, (p, c)))
    for _, action, args in sorted(plan, key=lambda entry: entry[0]):
        action(*args)

    rows_me = pl.ds(pl.multiple_of(i * WIDTH, WIDTH), WIDTH)
    for s in range(CAP):

        def deliver(d, carry):
            e = peer(d)
            send[s, e] = g16[chosen[e * CAP + s]]
            remote(
                send.at[s, e], mine.at[s, rows_me], g_s.at[s], g_r.at[s], e, m
            ).start()
            return carry

        lax.fori_loop(1, DP, deliver, 0)
        if s == 0:
            wait(mine.at[s, pl.ds(0, (DP - 1) * WIDTH)], g_s.at[s])
        mine[s, rows_me] = g16[chosen[i * CAP + s]]
    for copy in stat_copies:
        copy.wait()

    all_but_one = pl.ds(0, (DP - 1) * WIDTH)

    def refresh(s, carry):
        wait(mine.at[s, all_but_one], g_r.at[s])
        row = lax.broadcasted_iota(jnp.int32, (B, B), 0)
        col = lax.broadcasted_iota(jnp.int32, (B, B), 1)
        eye = jnp.where(row == col, 1.0, 0.0).astype(F32)
        grad = mine[s]
        wl, wl_rest = split(root_less_identity(lbuf[s] + dot(grad, grad, 1, 1), eye))
        wr, wr_rest = split(root_less_identity(rbuf[s] + dot(grad, grad, 0, 0), eye))
        half = grad.astype(F32) + (dot(wl, grad) + dot(wl_rest, grad))
        top, rest = split(half)
        full = half + (dot(top, wr) + (dot(rest, wr) + dot(top, wr_rest)))
        scale = lax.rsqrt(jnp.sum(full * full) * (1.0 / (B * B)) + 1e-06)
        upd[s] = (full * scale).astype(BF16)

        def give(d, inner):
            e = peer(d)
            rows = pl.ds(pl.multiple_of(e * WIDTH, WIDTH), WIDTH)
            remote(upd.at[s, rows], arr.at[s, i], u_s.at[s], u_r.at[s], e, m).start()
            return inner

        lax.fori_loop(1, DP, give, 0)
        arr[s, i] = upd[s, rows_me]
        return carry

    lax.fori_loop(0, CAP, refresh, 0)

    for s in range(CAP):
        wait(arr.at[s, pl.ds(0, DP - 1)], u_r.at[s])
    for j in range(NBLK):
        out[j] = arr[slot[j], owner[j]]

    for s in range(CAP):
        if s > 0:
            wait(mine.at[s, all_but_one], g_s.at[s])
        wait(mine.at[s, all_but_one], u_s.at[s])
    for c in range(GC):
        for d in range(1, NX):
            a_copy(c, d).wait_send()
            h_copy(c, d).wait_send()
        for q in range(NX):
            b1(c, 0, q).wait_send()
            b1(c, 1, q).wait_send()
            b2(c, q).wait_send()
            share(c, q).wait_send()
        for ring in range(2):
            for p in range(2):
                for k in range(4):
                    hop(ring, p, c, k).wait_send()


def body(hidden_acts, out_grads, left_stats, right_stats, block_owner, block_slot):
    hbm = pl.BlockSpec(memory_space=pl.ANY)
    smem = pl.BlockSpec(memory_space=pltpu.SMEM)
    vmem = pl.BlockSpec(memory_space=pltpu.VMEM)
    dma = pltpu.SemaphoreType.DMA
    result = pl.pallas_call(
        body_kernel,
        out_shape=jax.ShapeDtypeStruct((NBLK, WIDTH, B), BF16),
        in_specs=[hbm, hbm, hbm, hbm, smem, smem],
        out_specs=vmem,
        scratch_shapes=[
            pltpu.VMEM((GC, NX, MP, SUB, B), BF16),
            pltpu.VMEM((NX, TOK, GR * XROWS), BF16),
            pltpu.VMEM((GR * XROWS, NX * TOK), BF16),
            pltpu.VMEM((GC, NZ, GR, WIDTH, B), F32),
            pltpu.VMEM((GC, 3, GR, WIDTH, B), F32),
            pltpu.VMEM((GC, 3, GR, WIDTH, B), F32),
            pltpu.VMEM((2, GC, 2, GR, WIDTH, B), BF16),
            pltpu.VMEM((2, GC, 2, GR, WIDTH, B), BF16),
            pltpu.VMEM((NBLK, WIDTH, B), BF16),
            pltpu.VMEM((CAP, DP, WIDTH, B), BF16),
            pltpu.VMEM((CAP, B, B), BF16),
            pltpu.VMEM((CAP, B, B), BF16),
            pltpu.VMEM((CAP, DP, WIDTH, B), BF16),
            pltpu.VMEM((CAP, B, B), F32),
            pltpu.VMEM((CAP, B, B), F32),
            pltpu.SMEM((DP * CAP,), jnp.int32),
            dma((10,)),
            dma((GC, 3)), dma((GC, 3)),
            dma((GR, 3)), dma((GR, 3)),
            dma((GC, 2, NX)), dma((GC, 2, NX)),
            dma((GC, NX)), dma((GC, NX)),
            dma((GC, 4)), dma((GC, 4)),
            dma((2, 2, GC, 4)), dma((2, 2, GC, 4)),
            dma((CAP,)), dma((CAP,)),
            dma((CAP,)), dma((CAP,)),
        ],
        compiler_params=pltpu.CompilerParams(
            collective_id=0, has_side_effects=True, vmem_limit_bytes=60 * 1024 * 1024
        ),
        cost_estimate=pl.CostEstimate(
            flops=10 * 10**9, bytes_accessed=7 * 10**6, transcendentals=0
        ),
    )(hidden_acts, out_grads, left_stats, right_stats, block_owner, block_slot)
    return result[None]


def solution(mesh):
    in_specs = (
        P("dp", "mp"),
        P(("dp", "mp"), None),
        P("mp", "dp", None, None),
        P("mp", "dp", None, None),
        P(),
        P(),
    )
    out_specs = P("mp", None, "dp", None)
    return jax.shard_map(body, mesh=mesh, in_specs=in_specs, out_specs=out_specs, check_vma=False)
```

```python
import math

import jax
import jax.numpy as jnp
from jax import lax
from jax.experimental import pallas as pl
from jax.experimental.pallas import tpu as pltpu
from jax.sharding import PartitionSpec as P

B = 512
CAP = 2
NX = 4
NZ = 8
NY = 4
DP = NX * NZ
MP = 2 * NY
GR = 4
GC = 4
NBLK = GR * GC
TOK = 512
SUB = TOK // MP
WIDTH = B // DP
XROWS = B // NX
F32 = jnp.float32
BF16 = jnp.bfloat16
MESH = pl.DeviceIdType.MESH

A_TIMES = (0.0, 0.02, 0.04, 0.06)
OWN_TIMES = (0.01, 0.03, 0.05, 0.07)
H_TIMES = (7.5, 11.0, 13.05, 14.9)
FIND_TIME = 1.0
HID_TIME = 14.95
STAT_TIME = 55.0
RELAY_TIMES = (6.5, 6.65, 7.2, 7.4)
NEAR_TIMES = (6.6, 6.7, 12.2, 25.3)
FAR_TIMES = (9.5, 10.5, 13.05, 25.35)
MIDDLE_TIMES = (
    (8.0, 12.0, 12.1, 13.0), (10.6, 14.0, 14.1, 15.2),
    (27.0, 27.1, 27.2, 29.0), (29.1, 33.5, 33.6, 35.5),
)
LAST_TIMES = (19.0, 25.2, 33.0, 38.5)
PREPARE_TIMES = (23.0, 32.0)
TILES = (
    (24.0, 0, 0), (26.5, 0, 1), (32.1, 1, 0), (32.2, 1, 1),
    (35.0, 0, 2), (35.1, 1, 2), (41.0, 0, 3), (41.2, 1, 3),
)
HOP_TIMES = (0.37, 0.72, 0.72, 1.4)
HOP_DELAY = 2.4
LEAD = 1.0


def ring_order():
    waiting = [(t + 0.8, p, c, -1) for t, p, c in TILES]
    order, free, now = [], 0.0, 0.0
    while waiting:
        now = max(now, free - LEAD, min(waiting)[0])
        entry = min((e for e in waiting if e[0] <= now), key=lambda e: (e[3], e[0]))
        waiting.remove(entry)
        _, p, c, k = entry
        if k >= 0:
            order.append((now, p, c, k))
        if k < 3:
            free = max(now, free) + HOP_TIMES[k + 1]
            waiting.append((free + HOP_DELAY, p, c, k + 1))
    return order


def dot(a, b, ca=1, cb=0):
    return lax.dot_general(a, b, (((ca,), (cb,)), ((), ())), preferred_element_type=F32)


def split(value):
    top = value.astype(BF16)
    return top, (value - top.astype(F32)).astype(BF16)


def root_less_identity(matrix, eye):
    column_sums = jnp.sum(jnp.abs(matrix), axis=0, keepdims=True)
    scaling = 1.0 / (jnp.max(column_sums) + 1e-06)
    e1 = 0.25 * eye - (0.25 * scaling) * matrix
    e1b = e1.astype(BF16)
    e2 = dot(e1b, e1b)
    e2b = e2.astype(BF16)
    e34 = dot(e2b, (4.75 * e1 + e2).astype(BF16))
    return e1 + 2.5 * e2 + dot(e2b, (7.5 * e1 + 8.75 * e2 + e34).astype(BF16))


def body_kernel(
    hid, og, left, right, owner, slot, out,
    cg, hx, ht, tile, cw, ccw, early, landed, g16, send, mine, upd, arr, lbuf, rbuf, chosen,
    loc, a_s, a_r, h_s, h_r, b1_s, b1_r, b2_s, b2_r, s_s, s_r, r_s, r_r, g_s, g_r, u_s, u_r,
):
    i = lax.axis_index("dp")
    m = lax.axis_index("mp")
    x = i // NZ
    z = i % NZ
    core = m % 2
    sib = m + 1 - 2 * core
    up = (m + 2) % MP
    down = (m + MP - 2) % MP
    far = (m + 4) % MP
    factor = 1.0 / math.sqrt(B * TOK * DP)

    def remote(src, dst, ss, rs, dp, mp):
        return pltpu.make_async_remote_copy(
            src_ref=src, dst_ref=dst, send_sem=ss, recv_sem=rs,
            device_id=(dp, mp), device_id_type=MESH,
        )

    def wait(ref, sem):
        pltpu.make_async_copy(ref, ref, sem).wait()

    def peer(d):
        return ((x + d // NZ) % NX) * NZ + (z + d % NZ) % NZ

    def xpeer(d):
        return ((x + d) % NX) * NZ + z

    znext = x * NZ + (z + 1) % NZ
    zprev = x * NZ + (z + NZ - 1) % NZ

    def cols(r, xx):
        return pl.ds(pl.multiple_of(r * B + xx * XROWS, XROWS), XROWS)

    stat_copies = [
        pltpu.make_async_copy(left.at[0], lbuf, loc.at[0]),
        pltpu.make_async_copy(right.at[0], rbuf, loc.at[1]),
    ]
    own_copies = [
        pltpu.make_async_copy(og.at[:, pl.ds(c * B, B)], cg.at[c, x, m], loc.at[2 + c])
        for c in range(GC)
    ]
    hid_copies = [
        pltpu.make_async_copy(
            hid.at[:, cols(r, x)], hx.at[x, :, pl.ds(r * XROWS, XROWS)], loc.at[6 + r]
        )
        for r in range(GR)
    ]
    for copy in own_copies:
        copy.start()

    barrier = pltpu.get_barrier_semaphore()
    greeted = [(xpeer(d), m) for d in (1, 2, 3)]
    greeted += [(znext, m), (zprev, m), (i, up), (i, down), (i, sib)]
    for target in greeted:
        pl.semaphore_signal(barrier, inc=1, device_id=target, device_id_type=MESH)
    pl.semaphore_wait(barrier, len(greeted))

    def slab(q):
        return (x + q) % NX

    def a_copy(c, d):
        ss, rs = a_s.at[c, 3 - d], a_r.at[c, 3 - d]
        if d == 2:
            step = 1 + 2 * (c % 2)
            ref = cg.at[c, slab(4 - step), m]
            return remote(ref, ref, ss, rs, xpeer(step), m)
        return remote(og.at[:, pl.ds(c * B, B)], cg.at[c, x, m], ss, rs, xpeer(d), m)

    def h_copy(r, d):
        return remote(
            hid.at[:, cols(r, (x + d) % NX)], hx.at[x, :, pl.ds(r * XROWS, XROWS)],
            h_s.at[r, d - 1], h_r.at[r, d - 1], xpeer(d), m,
        )

    def b1(c, k, q):
        src = og.at[:, pl.ds(c * B, B)] if q == 0 else cg.at[c, slab(q), m]
        return remote(
            src, cg.at[c, slab(q), m], b1_s.at[c, k, q], b1_r.at[c, k, q], i, (up, down)[k]
        )

    def b2(c, q):
        k = q // 2
        ref = cg.at[c, slab(q), (down, up)[k]]
        return remote(ref, ref, b2_s.at[c, q], b2_r.at[c, q], i, (up, down)[k])

    def share(c, n):
        ref = cg.at[c, :, (m, down, up, far)[n]]
        return remote(ref, ref, s_s.at[c, n], s_r.at[c, n], i, sib)

    def send_a(c):
        for d in (1, 3):
            a_copy(c, d).start()

    def send_h(r):
        for d in (1, 3, 2):
            h_copy(r, d).start()

    def send_own(c):
        b1(c, 0, 0).start()
        b1(c, 1, 0).start()

    def relay(c):
        step = 1 + 2 * (c % 2)
        a_copy(c, step).wait_recv()
        a_copy(c, 2).start()

    def near(c):
        step = 1 + 2 * (c % 2)
        for d in (step, 4 - step):
            if d != step:
                a_copy(c, d).wait_recv()
            b1(c, 0, 4 - d).start()
            b1(c, 1, 4 - d).start()

    def far_one(c):
        a_copy(c, 2).wait_recv()
        b1(c, 0, 2).start()
        b1(c, 1, 2).start()
        own_copies[c].wait()
        share(c, 0).start()

    def middle(c, q):
        for k in (0, 1):
            b1(c, k, q).wait_recv()
            if k == q // 2:
                b2(c, q).start()
        if q == 2:
            share(c, 1).start()
            share(c, 2).start()

    def last(c):
        for q in range(NX):
            b2(c, q).wait_recv()
        share(c, 3).start()

    def prepare_hidden(p):
        for r in (2 * p, 2 * p + 1):
            hid_copies[r].wait()
            for d in (1, 3, 2):
                h_copy(r, d).wait_recv()
        half = pl.ds(2 * p * XROWS, 2 * XROWS)
        for n in range(NX):
            ht[half, pl.ds(n * TOK, TOK)] = hx[n, :, half].T

    def hop(ring, p, c, k):
        buf = (cw, ccw)[ring]
        target = (znext, zprev)[ring]
        ss, rs = r_s.at[ring, p, c, k], r_r.at[ring, p, c, k]
        if k < 3:
            rows = pl.ds(2 * p, 2) if k else 2 * p + ring
            return remote(
                early.at[ring, c, k, rows], landed.at[ring, c, k, rows], ss, rs, target, m
            )
        pair = pl.ds(2 * p, 2)
        return remote(buf.at[c, 0, pair], buf.at[c, 1, pair], ss, rs, target, m)

    seen = set()

    def multiply(p, c):
        if c not in seen:
            for n in range(4):
                share(c, n).wait_recv()
            seen.add(c)
        total = dot(ht[pl.ds(2 * p * XROWS, 2 * XROWS)], cg[c].reshape(NX * TOK, B))
        for r in range(2):
            for zz in range(NZ):
                start = r * XROWS + zz * WIDTH
                tile[c, zz, 2 * p + r] = total[start : start + WIDTH]
        for ring in (0, 1):
            row = 2 * p + ring
            early[ring, c, 0, row] = tile[c, (z + 4) % NZ, row].astype(BF16)
            hop(ring, p, c, 0).start()

    def ring_step(p, c, k):
        for ring in (0, 1):
            buf = (cw, ccw)[ring]
            hop(ring, p, c, k).wait_recv()
            chunk = (z + 3 - k) % NZ if ring == 0 else (z + NZ - 3 + k) % NZ
            pair = pl.ds(2 * p, 2)
            if k == 0:
                same, other = 2 * p + ring, 2 * p + 1 - ring
                summed = landed[ring, c, 0, same].astype(F32) + tile[c, chunk, same]
                early[ring, c, 1, same] = summed.astype(BF16)
                early[ring, c, 1, other] = tile[c, chunk, other].astype(BF16)
            elif k == 1:
                summed = landed[ring, c, 1, pair].astype(F32) + tile[c, chunk, pair]
                early[ring, c, 2, pair] = summed.astype(BF16)
            else:
                buf[c, 0, pair] = landed[ring, c, 2, pair].astype(F32) + tile[c, chunk, pair]
            hop(ring, p, c, k + 1).start()

    def ring_end(p, c):
        for ring in (0, 1):
            hop(ring, p, c, 3).wait_recv()
        pair = pl.ds(2 * p, 2)
        total = (tile[c, z, pair] + cw[c, 1, pair]) + ccw[c, 1, pair]
        total = (total * factor).astype(BF16)
        for r in range(2):
            g16[(2 * p + r) * GC + c] = total[r]

    def find_chosen():
        positions = [owner[j] * CAP + slot[j] for j in range(NBLK)]

        def find(p, carry):
            found = jnp.int32(0)
            for j in range(NBLK):
                found = jnp.where(positions[j] == p, j, found)
            chosen[p] = found
            return carry

        lax.fori_loop(0, DP * CAP, find, 0)

    def start_local(copies):
        for copy in copies:
            copy.start()

    plan = [(t, send_a, (c,)) for c, t in enumerate(A_TIMES)]
    plan += [(t, send_own, (c,)) for c, t in enumerate(OWN_TIMES)]
    plan += [(t, send_h, (r,)) for r, t in enumerate(H_TIMES)]
    plan += [(FIND_TIME, find_chosen, ()), (HID_TIME, start_local, (hid_copies,)), (STAT_TIME, start_local, (stat_copies,))]
    for c in range(GC):
        plan.append((RELAY_TIMES[c], relay, (c,)))
        plan.append((NEAR_TIMES[c], near, (c,)))
        plan.append((FAR_TIMES[c], far_one, (c,)))
        for q, t in zip((0, 3, 1, 2), MIDDLE_TIMES[c]):
            plan.append((t, middle, (c, q)))
        plan.append((LAST_TIMES[c], last, (c,)))
    plan += [(t, prepare_hidden, (p,)) for p, t in enumerate(PREPARE_TIMES)]
    for t, p, c in TILES:
        plan.append((t, multiply, (p, c)))
    for t, p, c, k in ring_order():
        plan.append((t, ring_step, (p, c, k)) if k < 3 else (t, ring_end, (p, c)))
    for _, action, args in sorted(plan, key=lambda entry: entry[0]):
        action(*args)

    rows_me = pl.ds(pl.multiple_of(i * WIDTH, WIDTH), WIDTH)
    for s in range(CAP):

        def deliver(d, carry):
            e = peer(d)
            send[s, e] = g16[chosen[e * CAP + s]]
            remote(
                send.at[s, e], mine.at[s, rows_me], g_s.at[s], g_r.at[s], e, m
            ).start()
            return carry

        lax.fori_loop(1, DP, deliver, 0)
        if s == 0:
            wait(mine.at[s, pl.ds(0, (DP - 1) * WIDTH)], g_s.at[s])
        mine[s, rows_me] = g16[chosen[i * CAP + s]]
    for copy in stat_copies:
        copy.wait()

    all_but_one = pl.ds(0, (DP - 1) * WIDTH)

    for c in range(GC):
        for d in range(1, NX):
            a_copy(c, d).wait_send()
            h_copy(c, d).wait_send()
        for q in range(NX):
            b1(c, 0, q).wait_send()
            b1(c, 1, q).wait_send()
            b2(c, q).wait_send()
            share(c, q).wait_send()
        for ring in range(2):
            for p in range(2):
                for k in range(4):
                    hop(ring, p, c, k).wait_send()

    def refresh(s, carry):
        wait(mine.at[s, all_but_one], g_r.at[s])
        row = lax.broadcasted_iota(jnp.int32, (B, B), 0)
        col = lax.broadcasted_iota(jnp.int32, (B, B), 1)
        eye = jnp.where(row == col, 1.0, 0.0).astype(F32)
        grad = mine[s]
        wl, wl_rest = split(root_less_identity(lbuf[s] + dot(grad, grad, 1, 1), eye))
        wr, wr_rest = split(root_less_identity(rbuf[s] + dot(grad, grad, 0, 0), eye))
        half = grad.astype(F32) + (dot(wl, grad) + dot(wl_rest, grad))
        top, rest = split(half)
        full = half + (dot(top, wr) + (dot(rest, wr) + dot(top, wr_rest)))
        scale = lax.rsqrt(jnp.sum(full * full) * (1.0 / (B * B)) + 1e-06)
        upd[s] = (full * scale).astype(BF16)

        def give(d, inner):
            e = peer(d)
            rows = pl.ds(pl.multiple_of(e * WIDTH, WIDTH), WIDTH)
            remote(upd.at[s, rows], arr.at[s, i], u_s.at[s], u_r.at[s], e, m).start()
            return inner

        lax.fori_loop(1, DP, give, 0)
        arr[s, i] = upd[s, rows_me]
        return carry

    lax.fori_loop(0, CAP, refresh, 0)

    for s in range(CAP):
        wait(arr.at[s, pl.ds(0, DP - 1)], u_r.at[s])
    for j in range(NBLK):
        out[j] = arr[slot[j], owner[j]]

    for s in range(CAP):
        if s > 0:
            wait(mine.at[s, all_but_one], g_s.at[s])
        wait(mine.at[s, all_but_one], u_s.at[s])


def body(hidden_acts, out_grads, left_stats, right_stats, block_owner, block_slot):
    hbm = pl.BlockSpec(memory_space=pl.ANY)
    smem = pl.BlockSpec(memory_space=pltpu.SMEM)
    vmem = pl.BlockSpec(memory_space=pltpu.VMEM)
    dma = pltpu.SemaphoreType.DMA
    result = pl.pallas_call(
        body_kernel,
        out_shape=jax.ShapeDtypeStruct((NBLK, WIDTH, B), BF16),
        in_specs=[hbm, hbm, hbm, hbm, smem, smem],
        out_specs=vmem,
        scratch_shapes=[
            pltpu.VMEM((GC, NX, MP, SUB, B), BF16),
            pltpu.VMEM((NX, TOK, GR * XROWS), BF16),
            pltpu.VMEM((GR * XROWS, NX * TOK), BF16),
            pltpu.VMEM((GC, NZ, GR, WIDTH, B), F32),
            pltpu.VMEM((GC, 2, GR, WIDTH, B), F32),
            pltpu.VMEM((GC, 2, GR, WIDTH, B), F32),
            pltpu.VMEM((2, GC, 3, GR, WIDTH, B), BF16),
            pltpu.VMEM((2, GC, 3, GR, WIDTH, B), BF16),
            pltpu.VMEM((NBLK, WIDTH, B), BF16),
            pltpu.VMEM((CAP, DP, WIDTH, B), BF16),
            pltpu.VMEM((CAP, B, B), BF16),
            pltpu.VMEM((CAP, B, B), BF16),
            pltpu.VMEM((CAP, DP, WIDTH, B), BF16),
            pltpu.VMEM((CAP, B, B), F32),
            pltpu.VMEM((CAP, B, B), F32),
            pltpu.SMEM((DP * CAP,), jnp.int32),
            dma((10,)),
            dma((GC, 3)), dma((GC, 3)),
            dma((GR, 3)), dma((GR, 3)),
            dma((GC, 2, NX)), dma((GC, 2, NX)),
            dma((GC, NX)), dma((GC, NX)),
            dma((GC, 4)), dma((GC, 4)),
            dma((2, 2, GC, 4)), dma((2, 2, GC, 4)),
            dma((CAP,)), dma((CAP,)),
            dma((CAP,)), dma((CAP,)),
        ],
        compiler_params=pltpu.CompilerParams(
            collective_id=0, has_side_effects=True, vmem_limit_bytes=60 * 1024 * 1024
        ),
        cost_estimate=pl.CostEstimate(
            flops=10 * 10**9, bytes_accessed=7 * 10**6, transcendentals=0
        ),
    )(hidden_acts, out_grads, left_stats, right_stats, block_owner, block_slot)
    return result[None]


def solution(mesh):
    in_specs = (
        P("dp", "mp"),
        P(("dp", "mp"), None),
        P("mp", "dp", None, None),
        P("mp", "dp", None, None),
        P(),
        P(),
    )
    out_specs = P("mp", None, "dp", None)
    return jax.shard_map(body, mesh=mesh, in_specs=in_specs, out_specs=out_specs, check_vma=False)
```

```python
import math

import jax
import jax.numpy as jnp
from jax import lax
from jax.experimental import pallas as pl
from jax.experimental.pallas import tpu as pltpu
from jax.sharding import PartitionSpec as P

B = 512
CAP = 2
NX = 4
NZ = 8
NY = 4
DP = NX * NZ
MP = 2 * NY
GR = 4
GC = 4
NBLK = GR * GC
TOK = 512
SUB = TOK // MP
WIDTH = B // DP
XROWS = B // NX
F32 = jnp.float32
BF16 = jnp.bfloat16
MESH = pl.DeviceIdType.MESH

A_TIMES = (0.0, 0.02, 0.04, 0.06)
OWN_TIMES = (0.01, 0.03, 0.05, 0.07)
H_TIMES = (7.5, 11.0, 13.05, 14.9)
FIND_TIME = 1.0
HID_TIME = 14.95
STAT_TIME = 55.0
RELAY_TIMES = (6.5, 6.65, 7.2, 7.4)
NEAR_TIMES = (6.6, 6.7, 12.2, 25.3)
FAR_TIMES = (9.5, 10.5, 13.05, 25.35)
MIDDLE_TIMES = (
    (8.0, 12.0, 12.1, 13.0), (10.6, 14.0, 14.1, 15.2),
    (27.0, 27.1, 27.2, 29.0), (29.1, 33.5, 33.6, 35.5),
)
LAST_TIMES = (19.0, 25.2, 33.0, 38.5)
PREPARE_TIMES = (23.0, 32.0)
TILES = (
    (24.0, 0, 0), (26.5, 0, 1), (32.1, 1, 0), (32.2, 1, 1),
    (35.0, 0, 2), (35.1, 1, 2), (41.0, 0, 3), (41.2, 1, 3),
)
HOP_TIMES = (0.37, 0.72, 0.72, 1.4)
HOP_DELAY = 2.4
LEAD = 1.0


def ring_order():
    waiting = [(t + 0.8, p, c, -1) for t, p, c in TILES]
    order, free, now = [], 0.0, 0.0
    while waiting:
        now = max(now, free - LEAD, min(waiting)[0])
        entry = min((e for e in waiting if e[0] <= now), key=lambda e: (e[3], e[0]))
        waiting.remove(entry)
        _, p, c, k = entry
        if k >= 0:
            order.append((now, p, c, k))
        if k < 3:
            free = max(now, free) + HOP_TIMES[k + 1]
            waiting.append((free + HOP_DELAY, p, c, k + 1))
    return order


def dot(a, b, ca=1, cb=0):
    return lax.dot_general(a, b, (((ca,), (cb,)), ((), ())), preferred_element_type=F32)


def split(value):
    top = value.astype(BF16)
    return top, (value - top.astype(F32)).astype(BF16)


def root_less_identity(matrix, eye):
    column_sums = jnp.sum(jnp.abs(matrix), axis=0, keepdims=True)
    scaling = 1.0 / (jnp.max(column_sums) + 1e-06)
    e1 = 0.25 * eye - (0.25 * scaling) * matrix
    e1b = e1.astype(BF16)
    e2 = dot(e1b, e1b)
    e2b = e2.astype(BF16)
    e34 = dot(e2b, (4.75 * e1 + e2).astype(BF16))
    return e1 + 2.5 * e2 + dot(e2b, (7.5 * e1 + 8.75 * e2 + e34).astype(BF16))


def body_kernel(
    hid, og, left, right, owner, slot, out,
    cg, hx, ht, tile, cw, ccw, early, landed, g16, send, mine, upd, arr, lbuf, rbuf, chosen,
    loc, a_s, a_r, h_s, h_r, b1_s, b1_r, b2_s, b2_r, s_s, s_r, r_s, r_r, g_s, g_r, u_s, u_r,
):
    i = lax.axis_index("dp")
    m = lax.axis_index("mp")
    x = i // NZ
    z = i % NZ
    core = m % 2
    sib = m + 1 - 2 * core
    up = (m + 2) % MP
    down = (m + MP - 2) % MP
    far = (m + 4) % MP
    factor = 1.0 / math.sqrt(B * TOK * DP)

    def remote(src, dst, ss, rs, dp, mp):
        return pltpu.make_async_remote_copy(
            src_ref=src, dst_ref=dst, send_sem=ss, recv_sem=rs,
            device_id=(dp, mp), device_id_type=MESH,
        )

    def wait(ref, sem):
        pltpu.make_async_copy(ref, ref, sem).wait()

    def peer(d):
        return ((x + d // NZ) % NX) * NZ + (z + d % NZ) % NZ

    def xpeer(d):
        return ((x + d) % NX) * NZ + z

    znext = x * NZ + (z + 1) % NZ
    zprev = x * NZ + (z + NZ - 1) % NZ

    def cols(r, xx):
        return pl.ds(pl.multiple_of(r * B + xx * XROWS, XROWS), XROWS)

    stat_copies = [
        pltpu.make_async_copy(left.at[0], lbuf, loc.at[0]),
        pltpu.make_async_copy(right.at[0], rbuf, loc.at[1]),
    ]
    own_copies = [
        pltpu.make_async_copy(og.at[:, pl.ds(c * B, B)], cg.at[c, x, m], loc.at[2 + c])
        for c in range(GC)
    ]
    hid_copies = [
        pltpu.make_async_copy(
            hid.at[:, cols(r, x)], hx.at[x, :, pl.ds(r * XROWS, XROWS)], loc.at[6 + r]
        )
        for r in range(GR)
    ]
    for copy in own_copies:
        copy.start()

    barrier = pltpu.get_barrier_semaphore()
    greeted = [(xpeer(d), m) for d in (1, 2, 3)]
    greeted += [(znext, m), (zprev, m), (i, up), (i, down), (i, sib)]
    for target in greeted:
        pl.semaphore_signal(barrier, inc=1, device_id=target, device_id_type=MESH)
    pl.semaphore_wait(barrier, len(greeted))

    def slab(q):
        return (x + q) % NX

    def a_copy(c, d):
        ss, rs = a_s.at[c, 3 - d], a_r.at[c, 3 - d]
        if d == 2:
            step = 1 + 2 * (c % 2)
            ref = cg.at[c, slab(4 - step), m]
            return remote(ref, ref, ss, rs, xpeer(step), m)
        return remote(og.at[:, pl.ds(c * B, B)], cg.at[c, x, m], ss, rs, xpeer(d), m)

    def h_copy(r, d):
        return remote(
            hid.at[:, cols(r, (x + d) % NX)], hx.at[x, :, pl.ds(r * XROWS, XROWS)],
            h_s.at[r, d - 1], h_r.at[r, d - 1], xpeer(d), m,
        )

    def b1(c, k, q):
        src = og.at[:, pl.ds(c * B, B)] if q == 0 else cg.at[c, slab(q), m]
        return remote(
            src, cg.at[c, slab(q), m], b1_s.at[c, k, q], b1_r.at[c, k, q], i, (up, down)[k]
        )

    def b2(c, q):
        k = q // 2
        ref = cg.at[c, slab(q), (down, up)[k]]
        return remote(ref, ref, b2_s.at[c, q], b2_r.at[c, q], i, (up, down)[k])

    def share(c, n):
        ref = cg.at[c, :, (m, down, up, far)[n]]
        return remote(ref, ref, s_s.at[c, n], s_r.at[c, n], i, sib)

    def send_a(c):
        for d in (1, 3):
            a_copy(c, d).start()

    def send_h(r):
        for d in (1, 3, 2):
            h_copy(r, d).start()

    def send_own(c):
        b1(c, 0, 0).start()
        b1(c, 1, 0).start()

    def relay(c):
        step = 1 + 2 * (c % 2)
        a_copy(c, step).wait_recv()
        a_copy(c, 2).start()

    def near(c):
        step = 1 + 2 * (c % 2)
        for d in (step, 4 - step):
            if d != step:
                a_copy(c, d).wait_recv()
            b1(c, 0, 4 - d).start()
            b1(c, 1, 4 - d).start()

    def far_one(c):
        a_copy(c, 2).wait_recv()
        b1(c, 0, 2).start()
        b1(c, 1, 2).start()
        own_copies[c].wait()
        share(c, 0).start()

    def middle(c, q):
        for k in (0, 1):
            b1(c, k, q).wait_recv()
            if k == q // 2:
                b2(c, q).start()
        if q == 2:
            share(c, 1).start()
            share(c, 2).start()

    def last(c):
        for q in range(NX):
            b2(c, q).wait_recv()
        share(c, 3).start()

    def prepare_hidden(p):
        for r in (2 * p, 2 * p + 1):
            hid_copies[r].wait()
            for d in (1, 3, 2):
                h_copy(r, d).wait_recv()
        half = pl.ds(2 * p * XROWS, 2 * XROWS)
        for n in range(NX):
            ht[half, pl.ds(n * TOK, TOK)] = hx[n, :, half].T

    def hop(ring, p, c, k):
        buf = (cw, ccw)[ring]
        target = (znext, zprev)[ring]
        ss, rs = r_s.at[ring, p, c, k], r_r.at[ring, p, c, k]
        if k < 3:
            rows = pl.ds(2 * p, 2) if k else 2 * p + ring
            return remote(
                early.at[ring, c, k, rows], landed.at[ring, c, k, rows], ss, rs, target, m
            )
        pair = pl.ds(2 * p, 2)
        return remote(buf.at[c, 0, pair], buf.at[c, 1, pair], ss, rs, target, m)

    seen = set()

    def multiply(p, c):
        if c not in seen:
            for n in range(4):
                share(c, n).wait_recv()
            seen.add(c)
        total = dot(ht[pl.ds(2 * p * XROWS, 2 * XROWS)], cg[c].reshape(NX * TOK, B))
        for r in range(2):
            for zz in range(NZ):
                start = r * XROWS + zz * WIDTH
                tile[c, zz, 2 * p + r] = total[start : start + WIDTH]
        for ring in (0, 1):
            row = 2 * p + ring
            early[ring, c, 0, row] = tile[c, (z + 4) % NZ, row].astype(BF16)
            hop(ring, p, c, 0).start()

    def ring_step(p, c, k):
        for ring in (0, 1):
            buf = (cw, ccw)[ring]
            hop(ring, p, c, k).wait_recv()
            chunk = (z + 3 - k) % NZ if ring == 0 else (z + NZ - 3 + k) % NZ
            pair = pl.ds(2 * p, 2)
            if k == 0:
                same, other = 2 * p + ring, 2 * p + 1 - ring
                summed = landed[ring, c, 0, same].astype(F32) + tile[c, chunk, same]
                early[ring, c, 1, same] = summed.astype(BF16)
                early[ring, c, 1, other] = tile[c, chunk, other].astype(BF16)
            elif k == 1:
                summed = landed[ring, c, 1, pair].astype(F32) + tile[c, chunk, pair]
                early[ring, c, 2, pair] = summed.astype(BF16)
            else:
                buf[c, 0, pair] = landed[ring, c, 2, pair].astype(F32) + tile[c, chunk, pair]
            hop(ring, p, c, k + 1).start()

    def ring_end(p, c):
        for ring in (0, 1):
            hop(ring, p, c, 3).wait_recv()
        pair = pl.ds(2 * p, 2)
        total = (tile[c, z, pair] + cw[c, 1, pair]) + ccw[c, 1, pair]
        total = (total * factor).astype(BF16)
        for r in range(2):
            g16[(2 * p + r) * GC + c] = total[r]

    def find_chosen():
        positions = [owner[j] * CAP + slot[j] for j in range(NBLK)]

        def find(p, carry):
            found = jnp.int32(0)
            for j in range(NBLK):
                found = jnp.where(positions[j] == p, j, found)
            chosen[p] = found
            return carry

        lax.fori_loop(0, DP * CAP, find, 0)

    def start_local(copies):
        for copy in copies:
            copy.start()

    plan = [(t, send_a, (c,)) for c, t in enumerate(A_TIMES)]
    plan += [(t, send_own, (c,)) for c, t in enumerate(OWN_TIMES)]
    plan += [(t, send_h, (r,)) for r, t in enumerate(H_TIMES)]
    plan += [(FIND_TIME, find_chosen, ()), (HID_TIME, start_local, (hid_copies,)), (STAT_TIME, start_local, (stat_copies,))]
    for c in range(GC):
        plan.append((RELAY_TIMES[c], relay, (c,)))
        plan.append((NEAR_TIMES[c], near, (c,)))
        plan.append((FAR_TIMES[c], far_one, (c,)))
        for q, t in zip((0, 3, 1, 2), MIDDLE_TIMES[c]):
            plan.append((t, middle, (c, q)))
        plan.append((LAST_TIMES[c], last, (c,)))
    plan += [(t, prepare_hidden, (p,)) for p, t in enumerate(PREPARE_TIMES)]
    for t, p, c in TILES:
        plan.append((t, multiply, (p, c)))
    for t, p, c, k in ring_order():
        plan.append((t, ring_step, (p, c, k)) if k < 3 else (t, ring_end, (p, c)))
    for _, action, args in sorted(plan, key=lambda entry: entry[0]):
        action(*args)

    rows_me = pl.ds(pl.multiple_of(i * WIDTH, WIDTH), WIDTH)
    for s in range(CAP):

        def deliver(d, carry):
            e = peer(d)
            send[s, e] = g16[chosen[e * CAP + s]]
            remote(
                send.at[s, e], mine.at[s, rows_me], g_s.at[s], g_r.at[s], e, m
            ).start()
            return carry

        lax.fori_loop(1, DP, deliver, 0)
        mine[s, rows_me] = g16[chosen[i * CAP + s]]
    for copy in stat_copies:
        copy.wait()

    all_but_one = pl.ds(0, (DP - 1) * WIDTH)

    for c in range(GC):
        for d in range(1, NX):
            a_copy(c, d).wait_send()
            h_copy(c, d).wait_send()
        for q in range(NX):
            b1(c, 0, q).wait_send()
            b1(c, 1, q).wait_send()
            b2(c, q).wait_send()
            share(c, q).wait_send()
        for ring in range(2):
            for p in range(2):
                for k in range(4):
                    hop(ring, p, c, k).wait_send()

    def refresh(s, carry):
        wait(mine.at[s, all_but_one], g_r.at[s])
        row = lax.broadcasted_iota(jnp.int32, (B, B), 0)
        col = lax.broadcasted_iota(jnp.int32, (B, B), 1)
        eye = jnp.where(row == col, 1.0, 0.0).astype(F32)
        grad = mine[s]
        wl, wl_rest = split(root_less_identity(lbuf[s] + dot(grad, grad, 1, 1), eye))
        wr, wr_rest = split(root_less_identity(rbuf[s] + dot(grad, grad, 0, 0), eye))
        half = grad.astype(F32) + (dot(wl, grad) + dot(wl_rest, grad))
        top, rest = split(half)
        full = half + (dot(top, wr) + (dot(rest, wr) + dot(top, wr_rest)))
        scale = lax.rsqrt(jnp.sum(full * full) * (1.0 / (B * B)) + 1e-06)
        upd[s] = (full * scale).astype(BF16)

        def give(d, inner):
            e = peer(d)
            rows = pl.ds(pl.multiple_of(e * WIDTH, WIDTH), WIDTH)
            remote(upd.at[s, rows], arr.at[s, i], u_s.at[s], u_r.at[s], e, m).start()
            return inner

        lax.fori_loop(1, DP, give, 0)
        arr[s, i] = upd[s, rows_me]
        return carry

    lax.fori_loop(0, CAP, refresh, 0)

    for s in range(CAP):
        wait(arr.at[s, pl.ds(0, DP - 1)], u_r.at[s])
    for j in range(NBLK):
        out[j] = arr[slot[j], owner[j]]

    for s in range(CAP):
        wait(mine.at[s, all_but_one], g_s.at[s])
        wait(mine.at[s, all_but_one], u_s.at[s])


def body(hidden_acts, out_grads, left_stats, right_stats, block_owner, block_slot):
    hbm = pl.BlockSpec(memory_space=pl.ANY)
    smem = pl.BlockSpec(memory_space=pltpu.SMEM)
    vmem = pl.BlockSpec(memory_space=pltpu.VMEM)
    dma = pltpu.SemaphoreType.DMA
    result = pl.pallas_call(
        body_kernel,
        out_shape=jax.ShapeDtypeStruct((NBLK, WIDTH, B), BF16),
        in_specs=[hbm, hbm, hbm, hbm, smem, smem],
        out_specs=vmem,
        scratch_shapes=[
            pltpu.VMEM((GC, NX, MP, SUB, B), BF16),
            pltpu.VMEM((NX, TOK, GR * XROWS), BF16),
            pltpu.VMEM((GR * XROWS, NX * TOK), BF16),
            pltpu.VMEM((GC, NZ, GR, WIDTH, B), F32),
            pltpu.VMEM((GC, 2, GR, WIDTH, B), F32),
            pltpu.VMEM((GC, 2, GR, WIDTH, B), F32),
            pltpu.VMEM((2, GC, 3, GR, WIDTH, B), BF16),
            pltpu.VMEM((2, GC, 3, GR, WIDTH, B), BF16),
            pltpu.VMEM((NBLK, WIDTH, B), BF16),
            pltpu.VMEM((CAP, DP, WIDTH, B), BF16),
            pltpu.VMEM((CAP, B, B), BF16),
            pltpu.VMEM((CAP, B, B), BF16),
            pltpu.VMEM((CAP, DP, WIDTH, B), BF16),
            pltpu.VMEM((CAP, B, B), F32),
            pltpu.VMEM((CAP, B, B), F32),
            pltpu.SMEM((DP * CAP,), jnp.int32),
            dma((10,)),
            dma((GC, 3)), dma((GC, 3)),
            dma((GR, 3)), dma((GR, 3)),
            dma((GC, 2, NX)), dma((GC, 2, NX)),
            dma((GC, NX)), dma((GC, NX)),
            dma((GC, 4)), dma((GC, 4)),
            dma((2, 2, GC, 4)), dma((2, 2, GC, 4)),
            dma((CAP,)), dma((CAP,)),
            dma((CAP,)), dma((CAP,)),
        ],
        compiler_params=pltpu.CompilerParams(
            collective_id=0, has_side_effects=True, vmem_limit_bytes=60 * 1024 * 1024
        ),
        cost_estimate=pl.CostEstimate(
            flops=10 * 10**9, bytes_accessed=7 * 10**6, transcendentals=0
        ),
    )(hidden_acts, out_grads, left_stats, right_stats, block_owner, block_slot)
    return result[None]


def solution(mesh):
    in_specs = (
        P("dp", "mp"),
        P(("dp", "mp"), None),
        P("mp", "dp", None, None),
        P("mp", "dp", None, None),
        P(),
        P(),
    )
    out_specs = P("mp", None, "dp", None)
    return jax.shard_map(body, mesh=mesh, in_specs=in_specs, out_specs=out_specs, check_vma=False)
```
